128 devices in a mesh: row: 8 (over y, z_hi), col: 16 (over x, z_lo, core).
Axes of the slice: x: 4, y: 4, z: 4 (z_hi: 2, z_lo: 2; z = z_hi * 2 + z_lo), core: 2. Of those that a mesh axis runs over, the one named last changes fastest.
Arguments:
- queries: bfloat16 [64, 3072, 128], P('row', 'col'), may hold values from -48 to 48
- keys: bfloat16 [64, 3072, 128], P('row', 'col'), may hold values from -48 to 48
- values: bfloat16 [64, 3072, 128], P('row', 'col'), may hold values from -6 to 6
- gate_logits: bfloat16 [64, 3072, 128], P('row', 'col'), may hold values from -6 to 6
- out_grad: bfloat16 [64, 3072, 128], P('row', 'col'), may hold values from -96 to 96
- pair_bias: bfloat16 [4, 3072, 3072], P(None, 'col', 'row'), may hold values from -6 to 6
- residue_mask: int32 [3072], replicated, may hold values 0 or 1
- query_weight: bfloat16 [128, 128], replicated, may hold values from -0.5 to 0.5
- pair_cotangent: bfloat16 [64, 3072, 128], P('row', 'col'), may hold values from -6 to 6
- right_proj: bfloat16 [3072, 3072, 128], P('col', 'row'), may hold values from -0.109375 to 0.109375
Outputs:
- grad_queries: bfloat16 [64, 3072, 128], P('row', 'col')
- grad_keys: bfloat16 [64, 3072, 128], P('row', 'col')
- grad_values: bfloat16 [64, 3072, 128], P('row', 'col')
- grad_gate_logits: bfloat16 [64, 3072, 128], P('row', 'col')
- grad_bias: float32 [4, 3072, 3072], P(None, 'col', 'row')
- grad_left: bfloat16 [64, 3072, 128], P('col', 'row')
The draws below stay inside these ranges and needn't reach their ends.
All inputs are finite; a program needn't handle non-finite values.
Results may differ from the reference program's by a relative error of at most 0.039.
Values may be sent and summed in bfloat16 or wider, within the bound.
No kernel may reach another device: no remote copies, remote signals or barrier semaphores. Data moves between devices by JAX's collectives and lax.ppermute only.
A program may use at most 192 MiB of HBM per device.

```python
import math
import jax
import jax.numpy as jnp
from jax import lax

C = 128
HEADS = 4
HEAD_DIM = 32
RB = 8
CJ = 192
N = 3072
BAND = 64
N_ROW = 8
N_COL = 16


def drawn_parts(key):
    base_draw = jnp.clip(jax.random.normal(jax.random.fold_in(key, 101), (BAND, N, HEADS * HEAD_DIM), jnp.float32), -6.0, 6.0)
    return base_draw


def draw_keys(key, part):
    base_draw = drawn_parts(key)
    result = base_draw
    return result.astype(jnp.bfloat16)


def draw_queries(key, part):
    key = jax.random.fold_in(key, 2)
    own_draw = jnp.clip(jax.random.normal(key, (BAND, N, HEADS * HEAD_DIM), jnp.float32), -6.0, 6.0)
    return own_draw.astype(jnp.bfloat16)


def plant(values, stream_key, low, largest):
    shape = values.shape
    spot = [jax.random.randint(jax.random.fold_in(stream_key, axis), (), 0, shape[axis]) for axis in range(len(shape))]
    values = values.at[tuple(spot)].set(low)
    longest = shape.index(max(shape))
    spot[longest] = (spot[longest] + 1) % shape[longest]
    return values.at[tuple(spot)].set(largest)


def steps_of(own_key, extent, split, smallest, top_value):
    def one(dim, shards_of):
        steps = jax.random.uniform(jax.random.fold_in(jax.random.fold_in(own_key, 6), dim), (shards_of,), jnp.float32, smallest / len(split), top_value / len(split))
        return jnp.repeat(jnp.exp(steps), extent[dim] // shards_of).reshape((-1,) + (1,) * (len(extent) - dim - 1))

    loudness = one(*split[0])
    for cut in split[1:]:
        loudness = loudness * one(*cut)
    return loudness


def scatter_about(own_key, extent, spread, reach, cuts=(), kind=jnp.bfloat16):
    values = jax.random.normal(own_key, extent, jnp.float32) * spread
    if len(cuts) > 0:
        values = steps_of(own_key, extent, cuts, -0.22, 0.18) * values
    return jnp.clip(values, min=-reach, max=reach).astype(kind)


def setup_inputs(seed: int = 0) -> dict:
    streams_of = jax.random.split(jax.random.key(seed), 11)
    queries = draw_queries(jax.random.fold_in(streams_of[10], 71), 0)
    keys = draw_keys(jax.random.fold_in(streams_of[10], 71), 0)
    values = scatter_about(streams_of[2], (BAND, N, C), 1.0, 6.0, ((0, 8), (1, 16)))
    gate_logits = scatter_about(streams_of[3], (BAND, N, C), 1.0, 6.0, ((0, 8), (1, 16)))
    out_grad = scatter_about(streams_of[4], (BAND, N, C), 16.0, 96.0, ((0, 8), (1, 16)))
    pair_bias = scatter_about(streams_of[5], (HEADS, N, N), 1.0, 6.0, ((1, 16), (2, 8)))
    residue_mask = plant((jax.random.randint(streams_of[6], (N,), 0, 8) < 7).astype(jnp.int32), jax.random.fold_in(streams_of[6], 1), 0, 1)
    query_weight = scatter_about(streams_of[7], (C, C), C ** -0.5, 0.5)
    pair_cotangent = scatter_about(streams_of[8], (BAND, N, C), 1.0, 6.0, ((0, 8), (1, 16)))
    right_proj = scatter_about(streams_of[9], (N, N, C), N ** -0.5, 0.109375, ((0, 16), (1, 8)))
    return {"queries": queries, "keys": keys, "values": values, "gate_logits": gate_logits, "out_grad": out_grad, "pair_bias": pair_bias, "residue_mask": residue_mask, "query_weight": query_weight, "pair_cotangent": pair_cotangent, "right_proj": right_proj}


big_penalty = 1000000000.0

def rounded(tensor):
    return lax.optimization_barrier(tensor.astype(jnp.bfloat16)).astype(jnp.float32)

def attend_row(q_row, k_row, v_row, gate_row, cot_row, bias_plus):
    length = q_row.shape[0]
    score_scale = 1.0 / math.sqrt(HEAD_DIM)
    q_heads = q_row.astype(jnp.float32).reshape(length, HEADS, HEAD_DIM)
    k_heads = k_row.astype(jnp.float32).reshape(length, HEADS, HEAD_DIM)
    v_heads = v_row.astype(jnp.float32).reshape(length, HEADS, HEAD_DIM)
    scores = jnp.einsum('jhd,khd->hjk', q_heads, k_heads) * score_scale + bias_plus
    row_top = lax.optimization_barrier(jnp.max(scores, axis=-1, keepdims=True))
    exponent = jnp.exp(scores - row_top)
    soft_weights = exponent / lax.optimization_barrier(jnp.sum(exponent, axis=-1, keepdims=True))
    weights_b = rounded(soft_weights)
    attended = jnp.einsum('hjk,khd->jhd', weights_b, v_heads)
    gate_value = jax.nn.sigmoid(gate_row.astype(jnp.float32)).reshape(length, HEADS, HEAD_DIM)
    cot_heads = cot_row.astype(jnp.float32).reshape(length, HEADS, HEAD_DIM)
    gate_grad = (cot_heads * attended * gate_value * (1.0 - gate_value)).reshape(length, HEADS * HEAD_DIM).astype(jnp.bfloat16)
    d_out = rounded(cot_heads * gate_value)
    d_weights = jnp.einsum('jhd,khd->hjk', d_out, v_heads)
    row_delta = lax.optimization_barrier(jnp.sum(d_out * attended, axis=-1))
    d_scores = soft_weights * (d_weights - jnp.transpose(row_delta)[:, :, None])
    d_scores_b = rounded(d_scores)
    grad_q = (jnp.einsum('hjk,khd->jhd', d_scores_b, k_heads) * score_scale).reshape(length, HEADS * HEAD_DIM).astype(jnp.bfloat16)
    block_len = length // N_COL
    ds_blocks = d_scores_b.reshape(HEADS, N_COL, block_len, length)
    wb_blocks = weights_b.reshape(HEADS, N_COL, block_len, length)
    q_blocks = q_heads.reshape(N_COL, block_len, HEADS, HEAD_DIM)
    dout_blocks = d_out.reshape(N_COL, block_len, HEADS, HEAD_DIM)
    key_terms = jnp.einsum('hcjk,cjhd->ckhd', ds_blocks, q_blocks) * score_scale
    value_terms = jnp.einsum('hcjk,cjhd->ckhd', wb_blocks, dout_blocks)
    grad_k = lax.optimization_barrier(jnp.sum(rounded(key_terms), axis=0)).reshape(length, HEADS * HEAD_DIM).astype(jnp.bfloat16)
    grad_v = lax.optimization_barrier(jnp.sum(rounded(value_terms), axis=0)).reshape(length, HEADS * HEAD_DIM).astype(jnp.bfloat16)
    return (grad_q, gate_grad, grad_k, grad_v, d_scores)

def reference(queries, keys, values, gate_logits, out_grad, pair_bias, residue_mask, query_weight, pair_cotangent, right_proj):
    penalty = big_penalty * (residue_mask.astype(jnp.float32) - 1.0)
    bias_plus = pair_bias.astype(jnp.float32) + penalty[None, None, :]

    def as_blocks(tensor):
        return tensor.reshape(N_ROW, RB, N, C)

    def block_step(grand_total, row_block):

        def row_step(running, band_row):
            grad_q, gate_grad, grad_k, grad_v, d_scores = attend_row(*band_row, bias_plus)
            return (running + d_scores, (grad_q, gate_grad, grad_k, grad_v))
        running, results = lax.scan(row_step, jnp.zeros((HEADS, N, N), jnp.float32), row_block)
        return (grand_total + rounded(running), results)
    grad_bias, results = lax.scan(block_step, jnp.zeros((HEADS, N, N), jnp.float32), (as_blocks(queries), as_blocks(keys), as_blocks(values), as_blocks(gate_logits), as_blocks(out_grad)))
    grad_queries, grad_gates, grad_keys, grad_values = [piece.reshape(BAND, N, C) for piece in results]
    flat_grads = grad_queries.reshape(BAND * N, C)
    carried = (pair_cotangent.astype(jnp.float32) + jnp.dot(flat_grads, query_weight.T, preferred_element_type=jnp.float32).reshape(BAND, N, C)).astype(jnp.bfloat16)
    carried_blocks = jnp.transpose(carried.reshape(BAND, N_COL, CJ, C), (1, 0, 2, 3))
    right_blocks = right_proj.reshape(N_COL, CJ, N, C)

    def col_step(grand_total, col_pair):
        left_part, right_part = col_pair
        term = jnp.einsum('ijc,jkc->ikc', left_part.astype(jnp.float32), right_part.astype(jnp.float32))
        return (grand_total + rounded(term), None)
    left_total, _ = lax.scan(col_step, jnp.zeros((BAND, N, C), jnp.float32), (carried_blocks, right_blocks))
    return (grad_queries, grad_keys, grad_values, grad_gates, grad_bias, left_total.astype(jnp.bfloat16))
```

```python
import functools
import math

import jax
import jax.numpy as jnp
from jax import lax
from jax.experimental import pallas as pl
from jax.experimental.pallas import tpu as pltpu
from jax.sharding import PartitionSpec as P

F32 = jnp.float32
BF = jnp.bfloat16
NT = (((1,), (1,)), ((), ()))
NN = (((1,), (0,)), ((), ()))
LOG2E = 1.4426950408889634
VMEM_LIMIT = 60 * 1024 * 1024
big_penalty = 1000000000.0


def dot(a, b, dims=NN):
    return lax.dot_general(a, b, dims, preferred_element_type=F32)


def attention_kernel(h0, total_heads, first, last, tile, order_ref, *refs):
    q_ref, kv_ref, g_ref, do_ref, pc_ref, w_ref = refs[:6]
    bias_refs = refs[6:10]
    refs = refs[10:]
    head_start = h0 == 0
    if not first:
        acc_in, refs = refs[0], refs[1:]
    if head_start:
        gq_ref, gg_ref, dkt_out, dvt_out, acc_out = refs[:5]
        refs = refs[5:]
    else:
        gq_in, gg_in, dkt_in, dvt_in = refs[:4]
        gq_ref, gg_ref, dkv_ref, car_ref, acc_out = refs[4:9]
        refs = refs[9:]
    bias_s, s_s, e_s, qt_s, dot_s, dkt_s, dvt_s, gq_s, acc_s = refs
    h = pl.program_id(0)
    i = pl.program_id(1)
    ni, cj, chan = q_ref.shape
    heads = pl.num_programs(0)
    head = chan // total_heads
    n = bias_s.shape[1]
    kb = n // 8
    scale = 1.0 / math.sqrt(head)
    hh = h + h0

    @pl.when(i == 0)
    def _():
        for s in range(8):
            off = pl.multiple_of(order_ref[s] * kb, 128)
            bias_s[:, pl.ds(off, kb)] = bias_refs[s // 2][s % 2, 0].astype(F32) * math.sqrt(head)
        if first:
            acc_s[...] = jnp.zeros(acc_s.shape, F32)
        else:
            acc_s[...] = acc_in[0]

    lane = lax.broadcasted_iota(jnp.int32, (cj, chan), 1)
    mask = (lane >= hh * head) & (lane < (hh + 1) * head)
    q = q_ref[i]
    qh = jnp.where(mask, q, jnp.zeros_like(q))

    @pl.when(h == 0)
    def _():
        qt_s[i] = q.astype(F32).T.astype(BF)
        if head_start:
            gq_s[i] = jnp.zeros((cj, chan), F32)
            gg_ref[i] = jnp.zeros((cj, chan), BF)
        else:
            gq_s[i] = gq_in[i].astype(F32)
            gg_ref[i] = gg_in[i]

    def rows(base, t):
        lo = t * tile
        out = []
        while lo < (t + 1) * tile:
            b, r = lo // cj, lo % cj
            m = min(cj - r, (t + 1) * tile - lo)
            out.append(kv_ref[b, base + i, r : r + m, :])
            lo += m
        return out[0] if len(out) == 1 else jnp.concatenate(out, axis=0)

    def k_rows(t):
        return rows(0, t)

    def v_rows(t):
        return rows(ni, t)

    tiles = n // tile
    m = None
    for t in range(tiles):
        sl = slice(t * tile, (t + 1) * tile)
        s = dot(qh, k_rows(t), NT) + bias_s[:, sl]
        s_s[:, sl] = s
        for u in range(tile // 128):
            p = s[:, u * 128 : (u + 1) * 128]
            m = p if m is None else jnp.maximum(m, p)
    top = jnp.max(m, axis=1, keepdims=True)
    lsum = None
    att = None
    for t in range(tiles):
        sl = slice(t * tile, (t + 1) * tile)
        e = jnp.exp2((s_s[:, sl] - top) * (scale * LOG2E))
        for u in range(tile // 128):
            p = e[:, u * 128 : (u + 1) * 128]
            lsum = p if lsum is None else lsum + p
        eb = e.astype(BF)
        e_s[:, sl] = eb
        a = dot(eb, v_rows(t))
        att = a if att is None else att + a
    linv = 1.0 / jnp.sum(lsum, axis=1, keepdims=True)
    att = att * linv
    gate = jax.nn.sigmoid(g_ref[i].astype(F32))
    cot = do_ref[i].astype(F32)
    gg = (cot * att * gate * (1.0 - gate)).astype(BF)
    gg_ref[i] = jnp.where(mask, gg, gg_ref[i])
    d_out = (cot * gate).astype(BF).astype(F32)
    d_out = jnp.where(mask, d_out, 0.0)
    delta = jnp.sum(d_out * att, axis=1, keepdims=True) * linv
    d_out = d_out * linv
    dob = d_out.astype(BF)
    dot_s[...] = d_out.T.astype(BF)
    hs = pl.ds(pl.multiple_of(hh * head, head), head)
    do_t = dot_s[hs, :]
    q_t = qt_s[i, hs, :]
    ls = pl.ds(pl.multiple_of(h * head, head), head)
    dq = None
    for t in range(tiles):
        sl = slice(t * tile, (t + 1) * tile)
        dp = dot(dob, v_rows(t), NT) - delta
        eb = e_s[:, sl]
        ds = eb.astype(F32) * dp
        acc_s[:, sl] += ds
        dsb = ds.astype(BF)
        a = dot(dsb, k_rows(t))
        dq = a if dq is None else dq + a
        dkt_s[i, ls, sl] = dot(q_t, dsb) * scale
        dvt_s[i, ls, sl] = dot(do_t, eb)
    gq_s[i] = jnp.where(mask, dq * scale, gq_s[i])

    @pl.when(h == heads - 1)
    def _():
        gq = gq_s[i].astype(BF)
        gq_ref[i] = gq
        if head_start:
            dkt_out[i] = dkt_s[i].astype(BF)
            dvt_out[i] = dvt_s[i].astype(BF)
        else:
            car = pc_ref[i].astype(F32) + dot(gq, w_ref[...], NT)
            car_ref[i] = car.T.astype(BF)
            for b in range(n // 384):
                sl = slice(b * 384, (b + 1) * 384)
                for base, old, new in ((0, dkt_in, dkt_s), (ni, dvt_in, dvt_s)):
                    both = jnp.concatenate([old[i, :, sl].astype(F32), new[i, :, sl]], axis=0).T.astype(BF)
                    for c in range(384 // cj):
                        dkv_ref[(384 // cj) * b + c, base + i] = both[c * cj : (c + 1) * cj]

    @pl.when(i == pl.num_programs(1) - 1)
    def _():
        if last:
            for s in range(8):
                off = pl.multiple_of(order_ref[s] * kb, 128)
                acc_out[s, 0] = acc_s[:, pl.ds(off, kb)].astype(BF)
        else:
            acc_out[0] = acc_s[...]


def attention(order, q, kv, g, do, pc, w, biases, acc, earlier, h0, heads, total_heads, last, tile=512):
    ni, cj, chan = q.shape
    nb = kv.shape[0]
    n = nb * cj
    kb = n // 8
    part = heads * (chan // total_heads)
    first = acc is None
    sd = jax.ShapeDtypeStruct

    def whole(*shape):
        return pl.BlockSpec(shape, lambda h, i, r: (0,) * len(shape), pipeline_mode=pl.Buffered(1))

    per_row = whole(ni, cj, chan)
    in_specs = [per_row, whole(nb, 2 * ni, cj, chan), per_row, per_row, per_row, whole(chan, chan)]
    in_specs += [pl.BlockSpec((2, 1, cj, kb), lambda h, i, r: (0, h, 0, 0))] * 4
    ops = [q, kv, g, do, pc, w, *biases]
    if not first:
        in_specs.append(pl.BlockSpec((1, cj, n), lambda h, i, r: (h, 0, 0)))
        ops.append(acc)
    out_specs = [per_row, per_row]
    out_shape = [sd((ni, cj, chan), BF), sd((ni, cj, chan), BF)]
    if h0 == 0:
        out_specs += [whole(ni, part, n), whole(ni, part, n)]
        out_shape += [sd((ni, part, n), BF), sd((ni, part, n), BF)]
    else:
        in_specs += [per_row, per_row, whole(ni, chan - part, n), whole(ni, chan - part, n)]
        ops += earlier
        out_specs += [whole(nb, 2 * ni, cj, chan), whole(ni, chan, cj)]
        out_shape += [sd((nb, 2 * ni, cj, chan), BF), sd((ni, chan, cj), BF)]
    if last:
        out_specs.append(pl.BlockSpec((8, 1, cj, kb), lambda h, i, r: (0, h, 0, 0)))
        out_shape.append(sd((8, heads, cj, kb), BF))
    else:
        out_specs.append(pl.BlockSpec((1, cj, n), lambda h, i, r: (h, 0, 0)))
        out_shape.append(sd((heads, cj, n), F32))
    scratch = [
        pltpu.VMEM((cj, n), F32),
        pltpu.VMEM((cj, n), F32),
        pltpu.VMEM((cj, n), BF),
        pltpu.VMEM((ni, chan, cj), BF),
        pltpu.VMEM((chan, cj), BF),
        pltpu.VMEM((ni, part, n), F32),
        pltpu.VMEM((ni, part, n), F32),
        pltpu.VMEM((ni, cj, chan), F32),
        pltpu.VMEM((cj, n), F32),
    ]
    return pl.pallas_call(
        functools.partial(attention_kernel, h0, total_heads, first, last, tile),
        grid_spec=pltpu.PrefetchScalarGridSpec(
            num_scalar_prefetch=1, grid=(heads, ni), in_specs=in_specs, out_specs=out_specs, scratch_shapes=scratch
        ),
        out_shape=out_shape,
        compiler_params=pltpu.CompilerParams(
            dimension_semantics=("arbitrary", "arbitrary"), vmem_limit_bytes=VMEM_LIMIT
        ),
        cost_estimate=pl.CostEstimate(
            flops=16 * heads * ni * cj * n * chan, bytes_accessed=30_000_000, transcendentals=heads * ni * cj * n
        ),
        name="attention_rows",
    )(order, *ops)


def left_kernel(order_ref, *refs):
    car = refs[:4]
    r_ref, out_ref, l_s, o_s = refs[4:]
    step = pl.program_id(0)
    _, ni, chan, cj = car[0].shape
    cb, _, kk = r_ref.shape
    rows = 8 * ni
    half = ni // 2

    @pl.when(step == 0)
    def _():
        for s in range(8):
            for i in range(ni):
                base = (s * ni + i) * chan
                x = car[s // 2][s % 2, i].astype(F32)
                l_s[0, base : base + chan, :] = x[:, :128]
                l_s[1, base : base + chan, : cj - 128] = x[:, 128:]

    for u in range(cb):
        c = step * cb + u
        a = l_s[0, pl.ds(c, rows, stride=chan), :]
        b = l_s[1, pl.ds(c, rows, stride=chan), :][:, : cj - 128]
        res = dot(jnp.concatenate([a, b], axis=1).astype(BF), r_ref[u])
        for b in range(kk // 128):
            o_s[b, pl.ds(c, rows, stride=chan), :] = res[:, b * 128 : (b + 1) * 128]

    @pl.when(step == pl.num_programs(0) - 1)
    def _():
        for s in range(8):
            for i in range(ni):
                base = (s * ni + i) * chan
                for b in range(kk // 128):
                    out_ref[2 * order_ref[s] + i // half, i % half, b * 128 : (b + 1) * 128, :] = o_s[
                        b, base : base + chan, :
                    ].T.astype(BF)


def left_product(order, cars, right_t, cb=16):
    _, ni, chan, cj = cars[0].shape
    kk = right_t.shape[2]

    def whole(*shape):
        return pl.BlockSpec(shape, lambda t, r: (0,) * len(shape), pipeline_mode=pl.Buffered(1))

    return pl.pallas_call(
        left_kernel,
        grid_spec=pltpu.PrefetchScalarGridSpec(
            num_scalar_prefetch=1,
            grid=(chan // cb,),
            in_specs=[whole(2, ni, chan, cj)] * 4 + [pl.BlockSpec((cb, cj, kk), lambda t, r: (t, 0, 0))],
            out_specs=whole(16, ni // 2, kk, chan),
            scratch_shapes=[
                pltpu.VMEM((2, 8 * ni * chan, 128), F32),
                pltpu.VMEM((kk // 128, 8 * ni * chan, 128), F32),
            ],
        ),
        out_shape=jax.ShapeDtypeStruct((16, ni // 2, kk, chan), BF),
        compiler_params=pltpu.CompilerParams(dimension_semantics=("arbitrary",), vmem_limit_bytes=VMEM_LIMIT),
        cost_estimate=pl.CostEstimate(
            flops=40_000_000_000, bytes_accessed=30_000_000, transcendentals=0
        ),
        name="left_product",
    )(order, *cars, right_t)


def row_shift(x, dy):
    return lax.ppermute(x, "row", [(2 * y + z, 2 * ((y + dy) % 4) + z) for y in range(4) for z in range(2)])


def row_swap(x):
    return lax.ppermute(x, "row", [(r, r ^ 1) for r in range(8)])


def row_pair(x):
    return jnp.stack([x, row_swap(x)])


def row_gather(pair):
    return [pair] + [row_shift(pair, dy) for dy in (1, 2, 3)]


def row_scatter_sum(x):
    total = x[0:2].astype(F32)
    for dy in (1, 2, 3):
        total = total + row_shift(x[2 * dy : 2 * dy + 2], -dy).astype(F32)
    total = total.astype(BF)
    return total[0].astype(F32) + row_swap(total[1]).astype(F32)


def local(
    queries,
    keys,
    values,
    gate_logits,
    out_grad,
    pair_bias,
    residue_mask,
    query_weight,
    pair_cotangent,
    right_proj,
):
    total_heads = pair_bias.shape[0]
    kb = pair_bias.shape[2]
    rb = queries.shape[0]
    row = lax.axis_index("row")
    y, z = row // 2, row % 2
    order = jnp.stack([2 * ((y - s // 2 + 4) % 4) + (z ^ (s % 2)) for s in range(8)]).astype(jnp.int32)
    penalty = big_penalty * (lax.dynamic_slice_in_dim(residue_mask, row * kb, kb).astype(F32) - 1.0)
    bias = (pair_bias.astype(F32) + penalty[None, None, :]).astype(BF)
    hs = total_heads // 2
    pairs = row_pair(bias)
    biases = [row_gather(pairs[:, :hs]), row_gather(pairs[:, hs:])]
    right_t = jnp.transpose(right_proj, (2, 0, 1))

    quarter = rb // 4
    picks = [
        tuple(range(0, quarter)) + tuple(range(2 * quarter, 3 * quarter)),
        tuple(range(quarter, 2 * quarter)) + tuple(range(3 * quarter, rb)),
    ]

    def take(x, ids):
        return jnp.concatenate([x[ids[0] : ids[quarter - 1] + 1], x[ids[quarter] : ids[-1] + 1]])

    gathered = [
        lax.all_gather(jnp.concatenate([take(keys, ids), take(values, ids)]), "col", axis=0) for ids in picks
    ]
    accs = [None, None]
    outs = []
    for part, ids in enumerate(picks):
        rows = [take(a, ids) for a in (queries, gate_logits, out_grad, pair_cotangent)]
        earlier = None
        for half in range(2):
            res = attention(
                order, rows[0], gathered[part], rows[1], rows[2], rows[3], query_weight, biases[half],
                accs[half], earlier, half * hs, hs, total_heads, part == 1,
            )
            earlier = list(res[:4])
            accs[half] = res[4]
        gq, gg, dkv, car = res[:4]
        dkv_sum = lax.psum_scatter(dkv, "col", scatter_dimension=0)
        left = left_product(order, row_gather(row_pair(car)), right_t)
        left_sum = lax.psum_scatter(left, "col", scatter_dimension=0)
        outs.append((gq, gg, dkv_sum[: rb // 2], dkv_sum[rb // 2 :], left_sum))

    def untake(a, b):
        return jnp.concatenate([a[:quarter], b[:quarter], a[quarter:], b[quarter:]])

    gq, gg, dk, dv = [untake(a, b) for a, b in zip(outs[0][:4], outs[1][:4])]
    left = jnp.concatenate([outs[0][4], outs[1][4]])
    grad_bias = jnp.concatenate([row_scatter_sum(a) for a in accs])
    return (gq, dk, dv, gg, grad_bias, left)


def solution(mesh):
    in_specs = (
        P("row", "col", None),
        P("row", "col", None),
        P("row", "col", None),
        P("row", "col", None),
        P("row", "col", None),
        P(None, "col", "row"),
        P(),
        P(),
        P("row", "col", None),
        P("col", "row", None),
    )
    out_specs = (
        P("row", "col", None),
        P("row", "col", None),
        P("row", "col", None),
        P("row", "col", None),
        P(None, "col", "row"),
        P("col", "row", None),
    )
    return jax.shard_map(local, mesh=mesh, in_specs=in_specs, out_specs=out_specs, check_vma=False)
```

```python
import functools
import math

import jax
import jax.numpy as jnp
from jax import lax
from jax.experimental import pallas as pl
from jax.experimental.pallas import tpu as pltpu
from jax.sharding import PartitionSpec as P

F32 = jnp.float32
BF = jnp.bfloat16
NT = (((1,), (1,)), ((), ()))
NN = (((1,), (0,)), ((), ()))
LOG2E = 1.4426950408889634
VMEM_LIMIT = 60 * 1024 * 1024
big_penalty = 1000000000.0


def dot(a, b, dims=NN):
    return lax.dot_general(a, b, dims, preferred_element_type=F32)


def attention_kernel(h0, heads, total_heads, first, last, tile, order_ref, cols_ref, *refs):
    q_ref, k_ref, v_ref, g_ref, do_ref, pc_ref, w_ref = refs[:7]
    bias_refs = refs[7:11]
    refs = refs[11:]
    head_start = h0 == 0
    if not first:
        acc_in, refs = refs[0], refs[1:]
    if head_start:
        gq_ref, gg_ref, dkt_out, dvt_out, acc_out = refs[:5]
        refs = refs[5:]
    else:
        gq_in, gg_in, dkt_in, dvt_in = refs[:4]
        gq_ref, gg_ref, keep_ref, send_ref, car_ref, acc_out = refs[4:10]
        refs = refs[10:]
    bias_s, s_s, e_s, t_s = refs[:4]
    refs = refs[4:]
    if not head_start:
        dkt_s, dvt_s, kv_s = refs[:3]
        refs = refs[3:]
    acc_s = acc_out
    if last:
        acc_s = refs[0]
        refs = refs[1:]
    i = pl.program_id(0)
    _, cj, chan = q_ref.shape
    head = chan // total_heads
    n = bias_s.shape[2]
    kb = n // 8
    scale = 1.0 / math.sqrt(head)
    tiles = n // tile
    fetch = None
    if not first:
        fetch = pltpu.make_async_copy(acc_in, acc_s, refs[0])

    @pl.when(i == 0)
    def _():
        if first:
            acc_s[...] = jnp.zeros(acc_s.shape, F32)
        else:
            fetch.start()
        for h in range(heads):
            for s in range(8):
                off = pl.multiple_of(order_ref[s] * kb, 128)
                bias_s[h, :, pl.ds(off, kb)] = bias_refs[s // 2][s % 2, h].astype(F32) * math.sqrt(head)

    def rows(ref, t):
        lo = t * tile
        out = []
        while lo < (t + 1) * tile:
            b, r = lo // cj, lo % cj
            m = min(cj - r, (t + 1) * tile - lo)
            out.append(ref[b, 0, r : r + m, :])
            lo += m
        return out[0] if len(out) == 1 else jnp.concatenate(out, axis=0)

    def lanes(h):
        lane = lax.broadcasted_iota(jnp.int32, (cj, chan), 1)
        return (lane >= (h0 + h) * head) & (lane < (h0 + h + 1) * head)

    def part(h):
        return slice((h0 + h) * head, (h0 + h + 1) * head)

    q = q_ref[0]
    q_t = q.astype(F32).T.astype(BF)
    tops = []
    for h in range(heads):
        qh = jnp.where(lanes(h), q, jnp.zeros_like(q))
        m = None
        for t in range(tiles):
            sl = slice(t * tile, (t + 1) * tile)
            s = dot(qh, rows(k_ref, t), NT) + bias_s[h, :, sl]
            s_s[h, :, sl] = s
            for u in range(tile // 128):
                p = s[:, u * 128 : (u + 1) * 128]
                m = p if m is None else jnp.maximum(m, p)
        tops.append(jnp.max(m, axis=1, keepdims=True))
    gate = jax.nn.sigmoid(g_ref[0].astype(F32))
    cot = do_ref[0].astype(F32)
    d_all = (cot * gate).astype(BF).astype(F32)
    gfac = cot * gate * (1.0 - gate)
    att_all = None
    stats = []
    for h in range(heads):
        lsum = None
        att = None
        for t in range(tiles):
            sl = slice(t * tile, (t + 1) * tile)
            e = jnp.exp2((s_s[h, :, sl] - tops[h]) * (scale * LOG2E))
            for u in range(tile // 128):
                p = e[:, u * 128 : (u + 1) * 128]
                lsum = p if lsum is None else lsum + p
            eb = e.astype(BF)
            e_s[h, :, sl] = eb
            a = dot(eb, rows(v_ref, t))
            att = a if att is None else att + a
        linv = 1.0 / jnp.sum(lsum, axis=1, keepdims=True)
        att = jnp.where(lanes(h), att * linv, 0.0)
        att_all = att if att_all is None else att_all + att
        delta = jnp.sum(d_all * att, axis=1, keepdims=True) * linv
        d_out = jnp.where(lanes(h), d_all * linv, 0.0)
        stats.append((delta, d_out.astype(BF)))
        t_s[h] = d_out.T.astype(BF)
    gg = gfac * att_all
    if not head_start:
        gg = gg + gg_in[0].astype(F32)
    gg_ref[0] = gg.astype(BF)

    if not first:

        @pl.when(i == 0)
        def _():
            fetch.wait()

    dq_all = None if head_start else gq_in[0].astype(F32)
    for h in range(heads):
        delta, dob = stats[h]
        out = slice(h * head, (h + 1) * head)
        do_t = t_s[h, part(h), :]
        dq = None
        for t in range(tiles):
            sl = slice(t * tile, (t + 1) * tile)
            dp = dot(dob, rows(v_ref, t), NT) - delta
            eb = e_s[h, :, sl]
            ds = eb.astype(F32) * dp
            acc_s[h, :, sl] += ds
            dsb = ds.astype(BF)
            a = dot(dsb, rows(k_ref, t))
            dq = a if dq is None else dq + a
            dk = dot(q_t[part(h), :], dsb) * scale
            dv = dot(do_t, eb)
            if head_start:
                dkt_out[0, out, sl] = dk.astype(BF)
                dvt_out[0, out, sl] = dv.astype(BF)
            else:
                dkt_s[out, sl] = dk
                dvt_s[out, sl] = dv
        dq = jnp.where(lanes(h), dq * scale, 0.0)
        dq_all = dq if dq_all is None else dq_all + dq
    gq = dq_all.astype(BF)
    gq_ref[0] = gq
    if not head_start:
        car = pc_ref[0].astype(F32) + dot(gq, w_ref[...], NT)
        car_ref[0] = car.T.astype(BF)
        for b in range(n // 384):
            sl = slice(b * 384, (b + 1) * 384)
            for j, old, new in ((0, dkt_in, dkt_s), (1, dvt_in, dvt_s)):
                both = jnp.concatenate([old[0, :, sl].astype(F32), new[:, sl]], axis=0).T.astype(BF)
                for c in range(384 // cj):
                    kv_s[(384 // cj) * b + c, j] = both[c * cj : (c + 1) * cj]
        half = n // cj // 2
        for r in range(half):
            keep_ref[r, 0] = kv_s[cols_ref[r]]
            send_ref[r, 0] = kv_s[cols_ref[half + r]]

    if last:

        @pl.when(i == pl.num_programs(0) - 1)
        def _():
            for h in range(heads):
                for s in range(8):
                    off = pl.multiple_of(s * kb, 128)
                    acc_out[s, h] = acc_s[h, :, pl.ds(off, kb)].astype(BF)


def attention(order, cols, q, kv, g, do, pc, w, biases, acc, earlier, h0, heads, total_heads, last, tile=3072):
    ni, cj, chan = q.shape
    nb = kv.shape[0]
    n = nb * cj
    kb = n // 8
    part = heads * (chan // total_heads)
    first = acc is None
    sd = jax.ShapeDtypeStruct

    def whole(*shape):
        return pl.BlockSpec(shape, lambda i, *r: (0,) * len(shape), pipeline_mode=pl.Buffered(1))

    per_row = pl.BlockSpec((1, cj, chan), lambda i, *r: (i, 0, 0))
    per_t = pl.BlockSpec((1, part, n), lambda i, *r: (i, 0, 0))
    k_spec = pl.BlockSpec((nb, 1, cj, chan), lambda i, *r: (0, i, 0, 0))
    v_spec = pl.BlockSpec((nb, 1, cj, chan), lambda i, *r: (0, ni + i, 0, 0))
    in_specs = [per_row, k_spec, v_spec, per_row, per_row, per_row, whole(chan, chan)]
    in_specs += [whole(2, heads, cj, kb)] * 4
    ops = [q, kv, kv, g, do, pc, w, *biases]
    if not first:
        in_specs.append(pl.BlockSpec(memory_space=pl.ANY))
        ops.append(acc)
    out_specs = [per_row, per_row]
    out_shape = [sd((ni, cj, chan), BF), sd((ni, cj, chan), BF)]
    scratch = [
        pltpu.VMEM((heads, cj, n), F32),
        pltpu.VMEM((heads, cj, n), F32),
        pltpu.VMEM((heads, cj, n), BF),
        pltpu.VMEM((heads, chan, cj), BF),
    ]
    if h0 == 0:
        out_specs += [per_t, per_t]
        out_shape += [sd((ni, part, n), BF), sd((ni, part, n), BF)]
    else:
        in_specs += [per_row, per_row, per_t, per_t]
        ops += earlier
        half = nb // 2
        kv_out = pl.BlockSpec((half, 1, 2, cj, chan), lambda i, *r: (0, i, 0, 0, 0))
        out_specs += [kv_out, kv_out, pl.BlockSpec((1, chan, cj), lambda i, *r: (i, 0, 0))]
        out_shape += [sd((half, ni, 2, cj, chan), BF), sd((half, ni, 2, cj, chan), BF), sd((ni, chan, cj), BF)]
        scratch += [pltpu.VMEM((part, n), F32), pltpu.VMEM((part, n), F32), pltpu.VMEM((nb, 2, cj, chan), BF)]
    if last:
        out_specs.append(whole(8, heads, cj, kb))
        out_shape.append(sd((8, heads, cj, kb), BF))
        scratch.append(pltpu.VMEM((heads, cj, n), F32))
    else:
        out_specs.append(whole(heads, cj, n))
        out_shape.append(sd((heads, cj, n), F32))
    if not first:
        scratch.append(pltpu.SemaphoreType.DMA(()))
    return pl.pallas_call(
        functools.partial(attention_kernel, h0, heads, total_heads, first, last, tile),
        grid_spec=pltpu.PrefetchScalarGridSpec(
            num_scalar_prefetch=2, grid=(ni,), in_specs=in_specs, out_specs=out_specs, scratch_shapes=scratch
        ),
        out_shape=out_shape,
        compiler_params=pltpu.CompilerParams(dimension_semantics=("arbitrary",), vmem_limit_bytes=VMEM_LIMIT),
        cost_estimate=pl.CostEstimate(
            flops=16 * heads * ni * cj * n * chan, bytes_accessed=30_000_000, transcendentals=heads * ni * cj * n
        ),
        name="attention_rows",
    )(order, cols, *ops)


def left_kernel(order_ref, cols_ref, *refs):
    car = refs[:4]
    r_ref, keep_ref, send_ref, l_s, o_s = refs[4:]
    step = pl.program_id(0)
    _, ni, chan, cj = car[0].shape
    cb, _, kk = r_ref.shape
    rows = 8 * ni
    half = ni // 2

    @pl.when(step == 0)
    def _():
        for s in range(8):
            for i in range(ni):
                at = pl.ds(pl.multiple_of((order_ref[s] * ni + i) * chan, chan), chan)
                x = car[s // 2][s % 2, i].astype(F32)
                l_s[0, at, :] = x[:, :128]
                l_s[1, at, : cj - 128] = x[:, 128:]

    for u in range(cb):
        c = step * cb + u
        a = l_s[0, pl.ds(c, rows, stride=chan), :]
        b = l_s[1, pl.ds(c, rows, stride=chan), :][:, : cj - 128]
        res = dot(jnp.concatenate([a, b], axis=1).astype(BF), r_ref[u])
        for b in range(kk // 128):
            o_s[b, pl.ds(c, rows, stride=chan), :] = res[:, b * 128 : (b + 1) * 128]

    @pl.when(step == pl.num_programs(0) - 1)
    def _():
        for r in range(8):
            for ref, col in ((keep_ref, cols_ref[r]), (send_ref, cols_ref[8 + r])):
                for i in range(half):
                    at = pl.ds(pl.multiple_of((col * half + i) * chan, chan), chan)
                    for b in range(kk // 128):
                        ref[r, i, b * 128 : (b + 1) * 128, :] = o_s[b, at, :].T.astype(BF)


def left_product(order, cols, cars, right_t, cb=16):
    _, ni, chan, cj = cars[0].shape
    kk = right_t.shape[2]

    def whole(*shape):
        return pl.BlockSpec(shape, lambda t, *r: (0,) * len(shape), pipeline_mode=pl.Buffered(1))

    return pl.pallas_call(
        left_kernel,
        grid_spec=pltpu.PrefetchScalarGridSpec(
            num_scalar_prefetch=2,
            grid=(chan // cb,),
            in_specs=[whole(2, ni, chan, cj)] * 4 + [pl.BlockSpec((cb, cj, kk), lambda t, *r: (t, 0, 0))],
            out_specs=[whole(8, ni // 2, kk, chan)] * 2,
            scratch_shapes=[
                pltpu.VMEM((2, 8 * ni * chan, 128), F32),
                pltpu.VMEM((kk // 128, 8 * ni * chan, 128), F32),
            ],
        ),
        out_shape=[jax.ShapeDtypeStruct((8, ni // 2, kk, chan), BF)] * 2,
        compiler_params=pltpu.CompilerParams(dimension_semantics=("arbitrary",), vmem_limit_bytes=VMEM_LIMIT),
        cost_estimate=pl.CostEstimate(
            flops=40_000_000_000, bytes_accessed=30_000_000, transcendentals=0
        ),
        name="left_product",
    )(order, cols, *cars, right_t)


def row_shift(x, dy):
    return lax.ppermute(x, "row", [(2 * y + z, 2 * ((y + dy) % 4) + z) for y in range(4) for z in range(2)])


def row_swap(x):
    return lax.ppermute(x, "row", [(r, r ^ 1) for r in range(8)])


def row_pair(x):
    return jnp.stack([x, row_swap(x)])


def row_gather(pair):
    return [pair] + [row_shift(pair, dy) for dy in (1, 2, 3)]


def row_sides(pair):
    return [row_shift(pair, 1), row_shift(pair, 3)]


def row_far(pair, side):
    back, on = side
    far = jnp.stack([row_shift(on[0], 3), row_shift(back[1], 1)])
    return [pair, back, far, on]


def add_all(parts):
    return sum(p.astype(F32) for p in parts).astype(BF)


def core_swap(send):
    return lax.ppermute(send, "col", [(c, c ^ 1) for c in range(16)])


def add_pair(a, b):
    return (a.astype(F32) + b.astype(F32)).astype(BF)


def core_sum(keep, send):
    return add_pair(keep, core_swap(send))


def x_shift(part, dx):
    return lax.ppermute(part[2 * dx : 2 * dx + 2], "col", [(c, (c + 4 * dx) % 16) for c in range(16)])


def z_swap(total):
    return lax.ppermute(total[1], "col", [(c, c ^ 2) for c in range(16)])


def z_sum(total):
    return add_pair(total[0], z_swap(total))


def after(x, *done):
    return lax.optimization_barrier((x, done))[0]


def local(
    queries,
    keys,
    values,
    gate_logits,
    out_grad,
    pair_bias,
    residue_mask,
    query_weight,
    pair_cotangent,
    right_proj,
):
    total_heads = pair_bias.shape[0]
    kb = pair_bias.shape[2]
    rb = queries.shape[0]
    row = lax.axis_index("row")
    y, z = row // 2, row % 2
    order = jnp.stack([2 * ((y - s // 2 + 4) % 4) + (z ^ (s % 2)) for s in range(8)]).astype(jnp.int32)
    col = lax.axis_index("col")
    x, zl, core = col // 4, (col // 2) % 2, col % 2
    cols = jnp.stack(
        [((x + r % 8 // 2) % 4) * 4 + (zl ^ (r % 2)) * 2 + (core ^ (r // 8)) for r in range(16)]
    ).astype(jnp.int32)
    penalty = big_penalty * (lax.dynamic_slice_in_dim(residue_mask, row * kb, kb).astype(F32) - 1.0)
    bias = (pair_bias.astype(F32) + penalty[None, None, :]).astype(BF)
    hs = total_heads // 2
    pairs = row_pair(bias)
    biases = [row_gather(pairs[:, :hs]), row_gather(pairs[:, hs:])]
    right_t = jnp.transpose(right_proj, (2, 0, 1))

    quarter = rb // 4
    picks = [
        tuple(range(0, quarter)) + tuple(range(2 * quarter, 3 * quarter)),
        tuple(range(quarter, 2 * quarter)) + tuple(range(3 * quarter, rb)),
    ]

    def take(x, ids):
        return jnp.concatenate([x[ids[0] : ids[quarter - 1] + 1], x[ids[quarter] : ids[-1] + 1]])

    gathered = [
        lax.all_gather(jnp.concatenate([take(keys, ids), take(values, ids)]), "col", axis=0) for ids in picks
    ]
    order, right_t = lax.optimization_barrier((order, right_t))
    small = [[take(a, ids) for a in (queries, gate_logits, out_grad, pair_cotangent)] for ids in picks]

    def attend(part, half, acc, earlier, order):
        q, g, do, pc = small[part]
        return attention(
            order, cols, q, gathered[part], g, do, pc, query_weight, biases[half],
            acc, earlier, half * hs, hs, total_heads, part == 1,
        )

    a = attend(0, 0, None, None, order)
    b = attend(0, 1, None, list(a[:4]), order)
    gq0, gg0, keep, send, car0 = b[:5]
    part0 = core_sum(keep, send)
    pair0 = row_pair(car0)
    order_c, part0, pair0 = lax.optimization_barrier((order, part0, pair0))
    near0 = [x_shift(part0, 1), x_shift(part0, 3)]
    side0 = row_sides(pair0)
    c = attend(1, 0, a[-1], None, order_c)
    near0, side0 = after((near0, side0), c[0])
    total0 = add_all([part0[0:2]] + near0)
    order_d, total0, side0 = lax.optimization_barrier((order, total0, side0))
    far0 = x_shift(part0, 2)
    cars0 = row_far(pair0, side0)
    d = attend(1, 1, b[-1], list(c[:4]), order_d)
    gq1, gg1, keep, send, car1 = d[:5]
    far0, cars0 = after((far0, cars0), gq1)
    total0 = add_all([total0, far0])
    order_l, total0, cars0, car1, send = lax.optimization_barrier((order, total0, cars0, car1, send))
    swap1 = row_swap(car1)
    got1 = core_swap(send)
    got_z0 = z_swap(total0)
    left0 = left_product(order_l, cols, cars0, right_t)
    swap1, got1, got_z0, left0 = lax.optimization_barrier((swap1, got1, got_z0, left0))
    dkv0 = add_pair(total0[0], got_z0)
    part1 = add_pair(keep, got1)
    pair1 = jnp.stack([car1, swap1])
    pair1, part1, left0 = lax.optimization_barrier((pair1, part1, left0))
    side1 = row_sides(pair1)
    got_l0 = core_swap(left0[1])
    near1 = [x_shift(part1, 1)]
    side1, got_l0 = lax.optimization_barrier((side1, got_l0))
    cars1 = row_far(pair1, side1)
    near1.append(x_shift(after(part1, got_l0), 3))
    far1 = x_shift(after(part1, cars1), 2)
    left1 = left_product(after(order, cars1), cols, cars1, right_t)
    near1, far1 = after((near1, far1), left1)
    part_l0 = add_pair(left0[0], after(got_l0, left1))
    total1 = add_all([part1[0:2], near1[0], near1[1], far1])
    total1, part_l0, left1 = lax.optimization_barrier((total1, part_l0, left1))
    dkv1 = z_sum(total1)
    part_l1 = core_sum(*left1)
    sums = [add_all([p[0:2], x_shift(p, 1), x_shift(p, 3), x_shift(p, 2)]) for p in (part_l0, part_l1)]
    left = z_sum(jnp.concatenate(sums, axis=1))
    bias_sum = [lax.psum_scatter(t[-1], "row", scatter_dimension=0).astype(F32) for t in (c, d)]

    def untake(a, b):
        return jnp.concatenate([a[:quarter], b[:quarter], a[quarter:], b[quarter:]])

    gq, gg = untake(gq0, gq1), untake(gg0, gg1)
    dk, dv = untake(dkv0[:, 0], dkv1[:, 0]), untake(dkv0[:, 1], dkv1[:, 1])
    return (gq, dk, dv, gg, jnp.concatenate(bias_sum), left)


def solution(mesh):
    in_specs = (
        P("row", "col", None),
        P("row", "col", None),
        P("row", "col", None),
        P("row", "col", None),
        P("row", "col", None),
        P(None, "col", "row"),
        P(),
        P(),
        P("row", "col", None),
        P("col", "row", None),
    )
    out_specs = (
        P("row", "col", None),
        P("row", "col", None),
        P("row", "col", None),
        P("row", "col", None),
        P(None, "col", "row"),
        P("col", "row", None),
    )
    return jax.shard_map(local, mesh=mesh, in_specs=in_specs, out_specs=out_specs, check_vma=False)
```

```python
import functools
import math

import jax
import jax.numpy as jnp
from jax import lax
from jax.experimental import pallas as pl
from jax.experimental.pallas import tpu as pltpu
from jax.sharding import PartitionSpec as P

F32 = jnp.float32
BF = jnp.bfloat16
NT = (((1,), (1,)), ((), ()))
NN = (((1,), (0,)), ((), ()))
LOG2E = 1.4426950408889634
VMEM_LIMIT = 60 * 1024 * 1024
big_penalty = 1000000000.0


def dot(a, b, dims=NN):
    return lax.dot_general(a, b, dims, preferred_element_type=F32)


def attention_kernel(h0, heads, total_heads, first, last, tile, order_ref, cols_ref, *refs):
    q_ref, k_ref, v_ref, g_ref, do_ref, pc_ref, w_ref = refs[:7]
    bias_refs = refs[7:15]
    refs = refs[15:]
    head_start = h0 == 0
    if not first:
        acc_in, refs = refs[0], refs[1:]
    if head_start:
        gq_ref, gg_ref, dkt_out, dvt_out, acc_out = refs[:5]
        refs = refs[5:]
    else:
        gq_in, gg_in, dkt_in, dvt_in = refs[:4]
        gq_ref, gg_ref, keep_ref, send_ref, car_ref, acc_out = refs[4:10]
        refs = refs[10:]
    bias_s, s_s, e_s, t_s = refs[:4]
    refs = refs[4:]
    if not head_start:
        dkt_s, dvt_s, kv_s = refs[:3]
        refs = refs[3:]
    acc_s = acc_out
    if last:
        acc_s = refs[0]
        refs = refs[1:]
    i = pl.program_id(0)
    _, cj, chan = q_ref.shape
    head = chan // total_heads
    n = bias_s.shape[2]
    kb = n // 8
    scale = 1.0 / math.sqrt(head)
    tiles = n // tile
    fetch = None
    if not first:
        fetch = pltpu.make_async_copy(acc_in, acc_s, refs[0])

    @pl.when(i == 0)
    def _():
        if first:
            acc_s[...] = jnp.zeros(acc_s.shape, F32)
        else:
            fetch.start()
        for h in range(heads):
            for s in range(8):
                off = pl.multiple_of(order_ref[s] * kb, 128)
                bias_s[h, :, pl.ds(off, kb)] = bias_refs[s][0, h].astype(F32) * math.sqrt(head)

    def rows(ref, t):
        lo = t * tile
        out = []
        while lo < (t + 1) * tile:
            b, r = lo // cj, lo % cj
            m = min(cj - r, (t + 1) * tile - lo)
            out.append(ref[b, 0, r : r + m, :])
            lo += m
        return out[0] if len(out) == 1 else jnp.concatenate(out, axis=0)

    def lanes(h):
        lane = lax.broadcasted_iota(jnp.int32, (cj, chan), 1)
        return (lane >= (h0 + h) * head) & (lane < (h0 + h + 1) * head)

    def part(h):
        return slice((h0 + h) * head, (h0 + h + 1) * head)

    q = q_ref[0]
    q_t = q.astype(F32).T.astype(BF)
    tops = []
    for h in range(heads):
        qh = jnp.where(lanes(h), q, jnp.zeros_like(q))
        m = None
        for t in range(tiles):
            sl = slice(t * tile, (t + 1) * tile)
            s = dot(qh, rows(k_ref, t), NT) + bias_s[h, :, sl]
            s_s[h, :, sl] = s
            for u in range(tile // 128):
                p = s[:, u * 128 : (u + 1) * 128]
                m = p if m is None else jnp.maximum(m, p)
        tops.append(jnp.max(m, axis=1, keepdims=True))
    gate = jax.nn.sigmoid(g_ref[0].astype(F32))
    cot = do_ref[0].astype(F32)
    d_all = (cot * gate).astype(BF).astype(F32)
    gfac = cot * gate * (1.0 - gate)
    att_all = None
    stats = []
    for h in range(heads):
        lsum = None
        att = None
        for t in range(tiles):
            sl = slice(t * tile, (t + 1) * tile)
            e = jnp.exp2((s_s[h, :, sl] - tops[h]) * (scale * LOG2E))
            for u in range(tile // 128):
                p = e[:, u * 128 : (u + 1) * 128]
                lsum = p if lsum is None else lsum + p
            eb = e.astype(BF)
            e_s[h, :, sl] = eb
            a = dot(eb, rows(v_ref, t))
            att = a if att is None else att + a
        linv = 1.0 / jnp.sum(lsum, axis=1, keepdims=True)
        att = jnp.where(lanes(h), att * linv, 0.0)
        att_all = att if att_all is None else att_all + att
        delta = jnp.sum(d_all * att, axis=1, keepdims=True) * linv
        d_out = jnp.where(lanes(h), d_all * linv, 0.0)
        stats.append((delta, d_out.astype(BF)))
        t_s[h] = d_out.T.astype(BF)
    gg = gfac * att_all
    if not head_start:
        gg = gg + gg_in[0].astype(F32)
    gg_ref[0] = gg.astype(BF)

    if not first:

        @pl.when(i == 0)
        def _():
            fetch.wait()

    dq_all = None if head_start else gq_in[0].astype(F32)
    for h in range(heads):
        delta, dob = stats[h]
        out = slice(h * head, (h + 1) * head)
        do_t = t_s[h, part(h), :]
        dq = None
        for t in range(tiles):
            sl = slice(t * tile, (t + 1) * tile)
            dp = dot(dob, rows(v_ref, t), NT) - delta
            eb = e_s[h, :, sl]
            ds = eb.astype(F32) * dp
            acc_s[h, :, sl] += ds
            dsb = ds.astype(BF)
            a = dot(dsb, rows(k_ref, t))
            dq = a if dq is None else dq + a
            dk = dot(q_t[part(h), :], dsb) * scale
            dv = dot(do_t, eb)
            if head_start:
                dkt_out[0, out, sl] = dk.astype(BF)
                dvt_out[0, out, sl] = dv.astype(BF)
            else:
                dkt_s[out, sl] = dk
                dvt_s[out, sl] = dv
        dq = jnp.where(lanes(h), dq * scale, 0.0)
        dq_all = dq if dq_all is None else dq_all + dq
    gq = dq_all.astype(BF)
    gq_ref[0] = gq
    if not head_start:
        car = pc_ref[0].astype(F32) + dot(gq, w_ref[...], NT)
        car_ref[0] = car.T.astype(BF)
        for b in range(n // 384):
            sl = slice(b * 384, (b + 1) * 384)
            for j, old, new in ((0, dkt_in, dkt_s), (1, dvt_in, dvt_s)):
                both = jnp.concatenate([old[0, :, sl].astype(F32), new[:, sl]], axis=0).T.astype(BF)
                for c in range(384 // cj):
                    kv_s[(384 // cj) * b + c, j] = both[c * cj : (c + 1) * cj]
        half = n // cj // 2
        for r in range(half):
            keep_ref[r, 0] = kv_s[cols_ref[r]]
            send_ref[r, 0] = kv_s[cols_ref[half + r]]

    if last:

        @pl.when(i == pl.num_programs(0) - 1)
        def _():
            for h in range(heads):
                for s in range(8):
                    off = pl.multiple_of((s if head_start else order_ref[s]) * kb, 128)
                    acc_out[s, h] = acc_s[h, :, pl.ds(off, kb)].astype(BF)


def attention(order, cols, q, kv, g, do, pc, w, biases, acc, earlier, h0, heads, total_heads, last, tile=3072):
    ni, cj, chan = q.shape
    nb = kv.shape[0]
    n = nb * cj
    kb = n // 8
    part = heads * (chan // total_heads)
    first = acc is None
    sd = jax.ShapeDtypeStruct

    def whole(*shape):
        return pl.BlockSpec(shape, lambda i, *r: (0,) * len(shape), pipeline_mode=pl.Buffered(1))

    per_row = pl.BlockSpec((1, cj, chan), lambda i, *r: (i, 0, 0))
    per_t = pl.BlockSpec((1, part, n), lambda i, *r: (i, 0, 0))
    k_spec = pl.BlockSpec((nb, 1, cj, chan), lambda i, *r: (0, i, 0, 0))
    v_spec = pl.BlockSpec((nb, 1, cj, chan), lambda i, *r: (0, ni + i, 0, 0))
    in_specs = [per_row, k_spec, v_spec, per_row, per_row, per_row, whole(chan, chan)]
    in_specs += [
        pl.BlockSpec((1, heads, cj, kb), lambda i, *r, z=z: (z, 0, 0, 0), pipeline_mode=pl.Buffered(1)) for _, z in biases
    ]
    ops = [q, kv, kv, g, do, pc, w, *(block for block, _ in biases)]
    if not first:
        in_specs.append(pl.BlockSpec(memory_space=pl.ANY))
        ops.append(acc)
    out_specs = [per_row, per_row]
    out_shape = [sd((ni, cj, chan), BF), sd((ni, cj, chan), BF)]
    scratch = [
        pltpu.VMEM((heads, cj, n), F32),
        pltpu.VMEM((heads, cj, n), F32),
        pltpu.VMEM((heads, cj, n), BF),
        pltpu.VMEM((heads, chan, cj), BF),
    ]
    if h0 == 0:
        out_specs += [per_t, per_t]
        out_shape += [sd((ni, part, n), BF), sd((ni, part, n), BF)]
    else:
        in_specs += [per_row, per_row, per_t, per_t]
        ops += earlier
        half = nb // 2
        kv_out = pl.BlockSpec((half, 1, 2, cj, chan), lambda i, *r: (0, i, 0, 0, 0))
        out_specs += [kv_out, kv_out, pl.BlockSpec((1, chan, cj), lambda i, *r: (i, 0, 0))]
        out_shape += [sd((half, ni, 2, cj, chan), BF), sd((half, ni, 2, cj, chan), BF), sd((ni, chan, cj), BF)]
        scratch += [pltpu.VMEM((part, n), F32), pltpu.VMEM((part, n), F32), pltpu.VMEM((nb, 2, cj, chan), BF)]
    if last:
        out_specs.append(whole(8, heads, cj, kb))
        out_shape.append(sd((8, heads, cj, kb), BF))
        scratch.append(pltpu.VMEM((heads, cj, n), F32))
    else:
        out_specs.append(whole(heads, cj, n))
        out_shape.append(sd((heads, cj, n), F32))
    if not first:
        scratch.append(pltpu.SemaphoreType.DMA(()))
    return pl.pallas_call(
        functools.partial(attention_kernel, h0, heads, total_heads, first, last, tile),
        grid_spec=pltpu.PrefetchScalarGridSpec(
            num_scalar_prefetch=2, grid=(ni,), in_specs=in_specs, out_specs=out_specs, scratch_shapes=scratch
        ),
        out_shape=out_shape,
        compiler_params=pltpu.CompilerParams(dimension_semantics=("arbitrary",), vmem_limit_bytes=VMEM_LIMIT),
        cost_estimate=pl.CostEstimate(
            flops=16 * heads * ni * cj * n * chan, bytes_accessed=30_000_000, transcendentals=heads * ni * cj * n
        ),
        name="attention_rows",
    )(order, cols, *ops)


def left_kernel(order_ref, cols_ref, *refs):
    car = refs[:8]
    r_ref, keep_ref, send_ref, l_s, o_s = refs[8:]
    step = pl.program_id(0)
    ni, chan, cj = car[0].shape
    cb, _, kk = r_ref.shape
    rows = 8 * ni
    half = ni // 2

    @pl.when(step == 0)
    def _():
        for s in range(8):
            for i in range(ni):
                at = pl.ds(pl.multiple_of((order_ref[s] * ni + i) * chan, chan), chan)
                x = car[s][i].astype(F32)
                l_s[0, at, :] = x[:, :128]
                l_s[1, at, : cj - 128] = x[:, 128:]

    for u in range(cb):
        c = step * cb + u
        a = l_s[0, pl.ds(c, rows, stride=chan), :]
        b = l_s[1, pl.ds(c, rows, stride=chan), :][:, : cj - 128]
        res = dot(jnp.concatenate([a, b], axis=1).astype(BF), r_ref[u])
        for b in range(kk // 128):
            o_s[b, pl.ds(c, rows, stride=chan), :] = res[:, b * 128 : (b + 1) * 128]

    @pl.when(step == pl.num_programs(0) - 1)
    def _():
        for r in range(8):
            for ref, col in ((keep_ref, cols_ref[r]), (send_ref, cols_ref[8 + r])):
                for i in range(half):
                    at = pl.ds(pl.multiple_of((col * half + i) * chan, chan), chan)
                    for b in range(kk // 128):
                        ref[r, i, b * 128 : (b + 1) * 128, :] = o_s[b, at, :].T.astype(BF)


def left_product(order, cols, cars, right_t, cb=16):
    ni, chan, cj = cars[0].shape
    kk = right_t.shape[2]

    def whole(*shape):
        return pl.BlockSpec(shape, lambda t, *r: (0,) * len(shape), pipeline_mode=pl.Buffered(1))

    return pl.pallas_call(
        left_kernel,
        grid_spec=pltpu.PrefetchScalarGridSpec(
            num_scalar_prefetch=2,
            grid=(chan // cb,),
            in_specs=[whole(ni, chan, cj)] * 8 + [pl.BlockSpec((cb, cj, kk), lambda t, *r: (t, 0, 0))],
            out_specs=[whole(8, ni // 2, kk, chan)] * 2,
            scratch_shapes=[
                pltpu.VMEM((2, 8 * ni * chan, 128), F32),
                pltpu.VMEM((kk // 128, 8 * ni * chan, 128), F32),
            ],
        ),
        out_shape=[jax.ShapeDtypeStruct((8, ni // 2, kk, chan), BF)] * 2,
        compiler_params=pltpu.CompilerParams(dimension_semantics=("arbitrary",), vmem_limit_bytes=VMEM_LIMIT),
        cost_estimate=pl.CostEstimate(
            flops=40_000_000_000, bytes_accessed=30_000_000, transcendentals=0
        ),
        name="left_product",
    )(order, cols, *cars, right_t)


def row_shift(x, dy):
    return lax.ppermute(x, "row", [(2 * y + z, 2 * ((y + dy) % 4) + z) for y in range(4) for z in range(2)])


def row_swap(x):
    return lax.ppermute(x, "row", [(r, r ^ 1) for r in range(8)])


def row_shifts(x):
    return [row_shift(x, dy) for dy in (1, 2, 3)]


def row_order(own, swapped, own_shifts, swapped_shifts):
    return [block for pair in zip([own] + own_shifts, [swapped] + swapped_shifts) for block in pair]


def row_parts(x):
    return [x[0:2]] + [row_shift(x[2 * dy : 2 * dy + 2], -dy) for dy in (1, 2, 3)]


def add_all(parts):
    return sum(p.astype(F32) for p in parts).astype(BF)


def core_swap(send):
    return lax.ppermute(send, "col", [(c, c ^ 1) for c in range(16)])


def add_pair(a, b):
    return (a.astype(F32) + b.astype(F32)).astype(BF)


def x_shift(part, dx):
    return lax.ppermute(part[2 * dx : 2 * dx + 2], "col", [(c, (c + 4 * dx) % 16) for c in range(16)])


def z_swap(total):
    return lax.ppermute(total[1], "col", [(c, c ^ 2) for c in range(16)])


def z_sum(total):
    return add_pair(total[0], z_swap(total))


def after(x, *done):
    return lax.optimization_barrier((x, done))[0]


def local(
    queries,
    keys,
    values,
    gate_logits,
    out_grad,
    pair_bias,
    residue_mask,
    query_weight,
    pair_cotangent,
    right_proj,
):
    total_heads = pair_bias.shape[0]
    kb = pair_bias.shape[2]
    rb = queries.shape[0]
    row = lax.axis_index("row")
    y, z = row // 2, row % 2
    order = jnp.stack([2 * ((y - s // 2 + 4) % 4) + (z ^ (s % 2)) for s in range(8)]).astype(jnp.int32)
    col = lax.axis_index("col")
    x, zl, core = col // 4, (col // 2) % 2, col % 2
    cols = jnp.stack(
        [((x + r % 8 // 2) % 4) * 4 + (zl ^ (r % 2)) * 2 + (core ^ (r // 8)) for r in range(16)]
    ).astype(jnp.int32)
    penalty = big_penalty * (lax.dynamic_slice_in_dim(residue_mask, row * kb, kb).astype(F32) - 1.0)
    bias = (pair_bias.astype(F32) + penalty[None, None, :]).astype(BF)
    hs = total_heads // 2
    bias_swap = row_swap(bias)
    first_shifts = row_shifts(bias[:hs])
    right_t = jnp.transpose(after(right_proj, bias_swap), (2, 0, 1))
    early = row_order(bias[:hs], bias_swap[:hs], first_shifts, row_shifts(bias_swap[:hs]))
    late = after(jnp.stack([bias[hs:], bias_swap[hs:]]), early)
    biases = [
        [(block[None], 0) for block in early],
        [(pair, z) for pair in [late] + row_shifts(late) for z in range(2)],
    ]

    quarter = rb // 4
    picks = [
        tuple(range(0, quarter)) + tuple(range(2 * quarter, 3 * quarter)),
        tuple(range(quarter, 2 * quarter)) + tuple(range(3 * quarter, rb)),
    ]

    def take(x, ids):
        return jnp.concatenate([x[ids[0] : ids[quarter - 1] + 1], x[ids[quarter] : ids[-1] + 1]])

    gathered = [
        lax.all_gather(jnp.concatenate([take(keys, ids), take(values, ids)]), "col", axis=0) for ids in picks
    ]
    order, right_t = lax.optimization_barrier((order, right_t))
    small = [[take(a, ids) for a in (queries, gate_logits, out_grad, pair_cotangent)] for ids in picks]

    def attend(part, half, acc, earlier, order):
        q, g, do, pc = small[part]
        return attention(
            order, cols, q, gathered[part], g, do, pc, query_weight, biases[half],
            acc, earlier, half * hs, hs, total_heads, part == 1,
        )

    a = attend(0, 0, None, None, order)
    b = attend(0, 1, None, list(a[:4]), order)
    gq0, gg0, keep, send, car0 = b[:5]
    got0, swap0, own0 = core_swap(send), row_swap(car0), row_shifts(car0)
    c = attend(1, 0, a[-1], None, after(order, gq0))
    got0, swap0, own0 = after((got0, swap0, own0), c[0])
    part0 = add_pair(keep, got0)
    part0, swap0 = lax.optimization_barrier((part0, swap0))
    near0 = [x_shift(part0, 1), x_shift(part0, 3)]
    swapped0 = row_shifts(swap0)
    d = attend(1, 1, b[-1], list(c[:4]), after(order, part0, c[0]))
    gq1, gg1, keep, send, car1 = d[:5]
    near0, swapped0 = after((near0, swapped0), gq1)
    total0 = add_all([part0[0:2]] + near0)
    order_l, car1, send = lax.optimization_barrier((order, car1, send))
    far0 = x_shift(part0, 2)
    swap1, own1, got1 = row_swap(car1), row_shifts(car1), core_swap(send)
    left0 = left_product(order_l, cols, row_order(car0, swap0, own0, swapped0), right_t)
    far0, swap1, own1, got1, left0 = lax.optimization_barrier((far0, swap1, own1, got1, left0))
    part1 = add_pair(keep, got1)
    swapped1 = row_shifts(swap1)
    total0 = add_all([total0, far0])
    part1, total0 = lax.optimization_barrier((part1, total0))
    near1 = [x_shift(part1, 1), x_shift(part1, 3)]
    got_l0 = core_swap(left0[1])
    swapped1, got_l0, total0, part1, bias1 = lax.optimization_barrier((swapped1, got_l0, total0, part1, d[-1]))
    bias1 = row_parts(bias1)
    part_l0 = add_pair(left0[0], got_l0)
    far1, got_z0 = x_shift(part1, 2), z_swap(total0)
    left1 = left_product(after(order, swapped1, near1), cols, row_order(car1, swap1, own1, swapped1), right_t)
    far1, got_z0, bias1 = after((far1, got_z0, bias1), left1)
    part_l0, left1 = lax.optimization_barrier((part_l0, left1))
    dkv0 = add_pair(total0[0], got_z0)
    got_l1 = core_swap(left1[1])
    sum_l0 = add_all([part_l0[0:2]] + [x_shift(part_l0, dx) for dx in (1, 3, 2)])
    dkv1 = z_sum(add_all([part1[0:2], far1] + near1))
    part_l1 = add_pair(left1[0], got_l1)
    bias1 = add_all(bias1)
    bias_z = row_swap(bias1[1])
    sum_l1 = add_all([part_l1[0:2]] + [x_shift(part_l1, dx) for dx in (1, 3, 2)])
    left = z_sum(jnp.concatenate([sum_l0, sum_l1], axis=1))
    bias0 = after(lax.psum_scatter(c[-1], "row", scatter_dimension=0), left)
    grad_bias = jnp.concatenate([bias0.astype(F32), bias1[0].astype(F32) + bias_z.astype(F32)])

    def untake(a, b):
        return jnp.concatenate([a[:quarter], b[:quarter], a[quarter:], b[quarter:]])

    gq, gg = untake(gq0, gq1), untake(gg0, gg1)
    dk, dv = untake(dkv0[:, 0], dkv1[:, 0]), untake(dkv0[:, 1], dkv1[:, 1])
    return (gq, dk, dv, gg, grad_bias, left)


def solution(mesh):
    in_specs = (
        P("row", "col", None),
        P("row", "col", None),
        P("row", "col", None),
        P("row", "col", None),
        P("row", "col", None),
        P(None, "col", "row"),
        P(),
        P(),
        P("row", "col", None),
        P("col", "row", None),
    )
    out_specs = (
        P("row", "col", None),
        P("row", "col", None),
        P("row", "col", None),
        P("row", "col", None),
        P(None, "col", "row"),
        P("col", "row", None),
    )
    return jax.shard_map(local, mesh=mesh, in_specs=in_specs, out_specs=out_specs, check_vma=False)
```

```python
import functools
import math

import jax
import jax.numpy as jnp
from jax import lax
from jax.experimental import pallas as pl
from jax.experimental.pallas import tpu as pltpu
from jax.sharding import PartitionSpec as P

F32 = jnp.float32
BF = jnp.bfloat16
NT = (((1,), (1,)), ((), ()))
NN = (((1,), (0,)), ((), ()))
LOG2E = 1.4426950408889634
VMEM_LIMIT = 60 * 1024 * 1024
big_penalty = 1000000000.0


def dot(a, b, dims=NN):
    return lax.dot_general(a, b, dims, preferred_element_type=F32)


def attention_kernel(h0, heads, total_heads, first, last, tile, order_ref, *refs):
    q_ref, k_ref, v_ref, g_ref, do_ref, pc_ref, w_ref = refs[:7]
    bias_refs = refs[7:15]
    refs = refs[15:]
    head_start = h0 == 0
    if not first:
        acc_in, refs = refs[0], refs[1:]
    if head_start:
        gq_ref, gg_ref, dkt_out, dvt_out, acc_out = refs[:5]
        refs = refs[5:]
    else:
        gq_in, gg_in, dkt_in, dvt_in = refs[:4]
        gq_ref, gg_ref, dkv_ref, car_ref, acc_out = refs[4:9]
        refs = refs[9:]
    bias_s, s_s, e_s, t_s = refs[:4]
    refs = refs[4:]
    if not head_start:
        dkt_s, dvt_s = refs[:2]
        refs = refs[2:]
    acc_s = acc_out
    if last:
        acc_s = refs[0]
        refs = refs[1:]
    i = pl.program_id(0)
    _, cj, chan = q_ref.shape
    head = chan // total_heads
    n = bias_s.shape[2]
    kb = n // 8
    scale = 1.0 / math.sqrt(head)
    tiles = n // tile
    fetch = None
    if not first:
        fetch = pltpu.make_async_copy(acc_in, acc_s, refs[0])

    @pl.when(i == 0)
    def _():
        if first:
            acc_s[...] = jnp.zeros(acc_s.shape, F32)
        else:
            fetch.start()
        for h in range(heads):
            for s in range(8):
                off = pl.multiple_of(order_ref[s] * kb, 128)
                bias_s[h, :, pl.ds(off, kb)] = bias_refs[s][0, h].astype(F32) * math.sqrt(head)

    def rows(ref, t):
        lo = t * tile
        out = []
        while lo < (t + 1) * tile:
            b, r = lo // cj, lo % cj
            m = min(cj - r, (t + 1) * tile - lo)
            out.append(ref[b, 0, r : r + m, :])
            lo += m
        return out[0] if len(out) == 1 else jnp.concatenate(out, axis=0)

    def lanes(h):
        lane = lax.broadcasted_iota(jnp.int32, (cj, chan), 1)
        return (lane >= (h0 + h) * head) & (lane < (h0 + h + 1) * head)

    def part(h):
        return slice((h0 + h) * head, (h0 + h + 1) * head)

    q = q_ref[0]
    q_t = q.astype(F32).T.astype(BF)
    tops = []
    for h in range(heads):
        qh = jnp.where(lanes(h), q, jnp.zeros_like(q))
        m = None
        for t in range(tiles):
            sl = slice(t * tile, (t + 1) * tile)
            s = dot(qh, rows(k_ref, t), NT) + bias_s[h, :, sl]
            s_s[h, :, sl] = s
            for u in range(tile // 128):
                p = s[:, u * 128 : (u + 1) * 128]
                m = p if m is None else jnp.maximum(m, p)
        tops.append(jnp.max(m, axis=1, keepdims=True))
    gate = jax.nn.sigmoid(g_ref[0].astype(F32))
    cot = do_ref[0].astype(F32)
    d_all = (cot * gate).astype(BF).astype(F32)
    gfac = cot * gate * (1.0 - gate)
    att_all = None
    stats = []
    for h in range(heads):
        lsum = None
        att = None
        for t in range(tiles):
            sl = slice(t * tile, (t + 1) * tile)
            e = jnp.exp2((s_s[h, :, sl] - tops[h]) * (scale * LOG2E))
            for u in range(tile // 128):
                p = e[:, u * 128 : (u + 1) * 128]
                lsum = p if lsum is None else lsum + p
            eb = e.astype(BF)
            e_s[h, :, sl] = eb
            a = dot(eb, rows(v_ref, t))
            att = a if att is None else att + a
        linv = 1.0 / jnp.sum(lsum, axis=1, keepdims=True)
        att = jnp.where(lanes(h), att * linv, 0.0)
        att_all = att if att_all is None else att_all + att
        delta = jnp.sum(d_all * att, axis=1, keepdims=True) * linv
        d_out = jnp.where(lanes(h), d_all * linv, 0.0)
        stats.append((delta, d_out.astype(BF)))
        t_s[h] = d_out.T.astype(BF)
    gg = gfac * att_all
    if not head_start:
        gg = gg + gg_in[0].astype(F32)
    gg_ref[0] = gg.astype(BF)

    if not first:

        @pl.when(i == 0)
        def _():
            fetch.wait()

    dq_all = None if head_start else gq_in[0].astype(F32)
    for h in range(heads):
        delta, dob = stats[h]
        out = slice(h * head, (h + 1) * head)
        do_t = t_s[h, part(h), :]
        dq = None
        for t in range(tiles):
            sl = slice(t * tile, (t + 1) * tile)
            dp = dot(dob, rows(v_ref, t), NT) - delta
            eb = e_s[h, :, sl]
            ds = eb.astype(F32) * dp
            acc_s[h, :, sl] += ds
            dsb = ds.astype(BF)
            a = dot(dsb, rows(k_ref, t))
            dq = a if dq is None else dq + a
            dk = dot(q_t[part(h), :], dsb) * scale
            dv = dot(do_t, eb)
            if head_start:
                dkt_out[0, out, sl] = dk.astype(BF)
                dvt_out[0, out, sl] = dv.astype(BF)
            else:
                dkt_s[out, sl] = dk
                dvt_s[out, sl] = dv
        dq = jnp.where(lanes(h), dq * scale, 0.0)
        dq_all = dq if dq_all is None else dq_all + dq
    gq = dq_all.astype(BF)
    gq_ref[0] = gq
    if not head_start:
        car = pc_ref[0].astype(F32) + dot(gq, w_ref[...], NT)
        car_ref[0] = car.T.astype(BF)
        for b in range(n // 384):
            sl = slice(b * 384, (b + 1) * 384)
            for j, old, new in ((0, dkt_in, dkt_s), (1, dvt_in, dvt_s)):
                both = jnp.concatenate([old[0, :, sl].astype(F32), new[:, sl]], axis=0).T.astype(BF)
                for c in range(384 // cj):
                    dkv_ref[(384 // cj) * b + c, j] = both[c * cj : (c + 1) * cj]

    if last:

        @pl.when(i == pl.num_programs(0) - 1)
        def _():
            for h in range(heads):
                for s in range(8):
                    off = pl.multiple_of(order_ref[s] * kb, 128)
                    acc_out[s, h] = acc_s[h, :, pl.ds(off, kb)].astype(BF)


def attention(order, q, kv, g, do, pc, w, biases, acc, earlier, h0, heads, total_heads, last, tile=3072):
    ni, cj, chan = q.shape
    nb = kv.shape[0]
    n = nb * cj
    kb = n // 8
    part = heads * (chan // total_heads)
    first = acc is None
    sd = jax.ShapeDtypeStruct

    def whole(*shape):
        return pl.BlockSpec(shape, lambda i, *r: (0,) * len(shape), pipeline_mode=pl.Buffered(1))

    per_row = pl.BlockSpec((1, cj, chan), lambda i, *r: (i, 0, 0))
    per_t = pl.BlockSpec((1, part, n), lambda i, *r: (i, 0, 0))
    k_spec = pl.BlockSpec((nb, 1, cj, chan), lambda i, *r: (0, i, 0, 0))
    v_spec = pl.BlockSpec((nb, 1, cj, chan), lambda i, *r: (0, ni + i, 0, 0))
    in_specs = [per_row, k_spec, v_spec, per_row, per_row, per_row, whole(chan, chan)]
    in_specs += [
        pl.BlockSpec((1, heads, cj, kb), lambda i, *r, z=z: (z, 0, 0, 0), pipeline_mode=pl.Buffered(1)) for _, z in biases
    ]
    ops = [q, kv, kv, g, do, pc, w, *(block for block, _ in biases)]
    if not first:
        in_specs.append(pl.BlockSpec(memory_space=pl.ANY))
        ops.append(acc)
    out_specs = [per_row, per_row]
    out_shape = [sd((ni, cj, chan), BF), sd((ni, cj, chan), BF)]
    scratch = [
        pltpu.VMEM((heads, cj, n), F32),
        pltpu.VMEM((heads, cj, n), F32),
        pltpu.VMEM((heads, cj, n), BF),
        pltpu.VMEM((heads, chan, cj), BF),
    ]
    if h0 == 0:
        out_specs += [per_t, per_t]
        out_shape += [sd((ni, part, n), BF), sd((ni, part, n), BF)]
    else:
        in_specs += [per_row, per_row, per_t, per_t]
        ops += earlier
        kv_out = pl.BlockSpec((nb, 2, cj, chan), lambda i, *r: (0, i, 0, 0))
        out_specs += [kv_out, pl.BlockSpec((1, chan, cj), lambda i, *r: (i, 0, 0))]
        out_shape += [sd((nb, 2 * ni, cj, chan), BF), sd((ni, chan, cj), BF)]
        scratch += [pltpu.VMEM((part, n), F32), pltpu.VMEM((part, n), F32)]
    if last:
        out_specs.append(whole(8, heads, cj, kb))
        out_shape.append(sd((8, heads, cj, kb), BF))
        scratch.append(pltpu.VMEM((heads, cj, n), F32))
    else:
        out_specs.append(whole(heads, cj, n))
        out_shape.append(sd((heads, cj, n), F32))
    if not first:
        scratch.append(pltpu.SemaphoreType.DMA(()))
    return pl.pallas_call(
        functools.partial(attention_kernel, h0, heads, total_heads, first, last, tile),
        grid_spec=pltpu.PrefetchScalarGridSpec(
            num_scalar_prefetch=1, grid=(ni,), in_specs=in_specs, out_specs=out_specs, scratch_shapes=scratch
        ),
        out_shape=out_shape,
        compiler_params=pltpu.CompilerParams(dimension_semantics=("arbitrary",), vmem_limit_bytes=VMEM_LIMIT),
        cost_estimate=pl.CostEstimate(
            flops=16 * heads * ni * cj * n * chan, bytes_accessed=30_000_000, transcendentals=heads * ni * cj * n
        ),
        name="attention_rows",
    )(order, *ops)


def left_kernel(rows, order_ref, cols_ref, *refs):
    car = refs[:8]
    r_ref, keep_ref, send_ref, l_s, o_s = refs[8:]
    step = pl.program_id(0)
    _, _, chan, cj = car[0].shape
    cb, _, kk = r_ref.shape
    ni = len(rows)
    half = ni // 2

    @pl.when(step == 0)
    def _():
        for s in range(8):
            for i in range(ni):
                at = pl.ds(pl.multiple_of((order_ref[s] * ni + i) * chan, chan), chan)
                x = car[s][0, rows[i]].astype(F32)
                l_s[0, at, :] = x[:, :128]
                l_s[1, at, : cj - 128] = x[:, 128:]

    for u in range(cb):
        c = step * cb + u
        a = l_s[0, pl.ds(c, 8 * ni, stride=chan), :]
        b = l_s[1, pl.ds(c, 8 * ni, stride=chan), :][:, : cj - 128]
        res = dot(jnp.concatenate([a, b], axis=1).astype(BF), r_ref[u])
        for b in range(kk // 128):
            o_s[b, pl.ds(c, 8 * ni, stride=chan), :] = res[:, b * 128 : (b + 1) * 128]

    @pl.when(step == pl.num_programs(0) - 1)
    def _():
        for r in range(8):
            for ref, col in ((keep_ref, cols_ref[r]), (send_ref, cols_ref[8 + r])):
                for i in range(half):
                    at = pl.ds(pl.multiple_of((col * half + i) * chan, chan), chan)
                    for b in range(kk // 128):
                        ref[r, i, b * 128 : (b + 1) * 128, :] = o_s[b, at, :].T.astype(BF)


def left_product(order, cols, pairs, right_t, rows, cb=16):
    _, total, chan, cj = pairs[0].shape
    ni = len(rows)
    kk = right_t.shape[2]

    def whole(*shape):
        return pl.BlockSpec(shape, lambda t, *r: (0,) * len(shape), pipeline_mode=pl.Buffered(1))

    cars = [
        pl.BlockSpec((1, total, chan, cj), lambda t, *r, z=z: (z, 0, 0, 0), pipeline_mode=pl.Buffered(1))
        for _ in pairs
        for z in range(2)
    ]
    return pl.pallas_call(
        functools.partial(left_kernel, rows),
        grid_spec=pltpu.PrefetchScalarGridSpec(
            num_scalar_prefetch=2,
            grid=(chan // cb,),
            in_specs=cars + [pl.BlockSpec((cb, cj, kk), lambda t, *r: (t, 0, 0))],
            out_specs=[whole(8, ni // 2, kk, chan)] * 2,
            scratch_shapes=[
                pltpu.VMEM((2, 8 * ni * chan, 128), F32),
                pltpu.VMEM((kk // 128, 8 * ni * chan, 128), F32),
            ],
        ),
        out_shape=[jax.ShapeDtypeStruct((8, ni // 2, kk, chan), BF)] * 2,
        compiler_params=pltpu.CompilerParams(dimension_semantics=("arbitrary",), vmem_limit_bytes=VMEM_LIMIT),
        cost_estimate=pl.CostEstimate(flops=40_000_000_000, bytes_accessed=30_000_000, transcendentals=0),
        name="left_product",
    )(order, cols, *(pair for pair in pairs for _ in range(2)), right_t)


def row_shift(x, dy):
    return lax.ppermute(x, "row", [(2 * y + z, 2 * ((y + dy) % 4) + z) for y in range(4) for z in range(2)])


def row_swap(x):
    return lax.ppermute(x, "row", [(r, r ^ 1) for r in range(8)])


def row_shifts(x):
    return [row_shift(x, dy) for dy in (1, 2, 3)]


def row_order(own, swapped, own_shifts, swapped_shifts):
    return [block for pair in zip([own] + own_shifts, [swapped] + swapped_shifts) for block in pair]


def row_parts(x):
    return [x[0:2]] + [row_shift(x[2 * dy : 2 * dy + 2], -dy) for dy in (1, 2, 3)]


def add_all(parts):
    return sum(p.astype(F32) for p in parts).astype(BF)


def core_swap(send):
    return lax.ppermute(send, "col", [(c, c ^ 1) for c in range(16)])


def add_pair(a, b):
    return (a.astype(F32) + b.astype(F32)).astype(BF)


def x_shift(part, dx):
    return lax.ppermute(part[2 * dx : 2 * dx + 2], "col", [(c, (c + 4 * dx) % 16) for c in range(16)])


def z_swap(total):
    return lax.ppermute(total[1], "col", [(c, c ^ 2) for c in range(16)])


def z_sum(total):
    return add_pair(total[0], z_swap(total))


def after(x, *done):
    return lax.optimization_barrier((x, done))[0]


def local(
    queries,
    keys,
    values,
    gate_logits,
    out_grad,
    pair_bias,
    residue_mask,
    query_weight,
    pair_cotangent,
    right_proj,
):
    total_heads = pair_bias.shape[0]
    kb = pair_bias.shape[2]
    rb = queries.shape[0]
    row = lax.axis_index("row")
    y, z = row // 2, row % 2
    order = jnp.stack([2 * ((y - s // 2 + 4) % 4) + (z ^ (s % 2)) for s in range(8)]).astype(jnp.int32)
    col = lax.axis_index("col")
    x, zl, core = col // 4, (col // 2) % 2, col % 2
    cols = jnp.stack(
        [((x + r % 8 // 2) % 4) * 4 + (zl ^ (r % 2)) * 2 + (core ^ (r // 8)) for r in range(16)]
    ).astype(jnp.int32)
    penalty = big_penalty * (lax.dynamic_slice_in_dim(residue_mask, row * kb, kb).astype(F32) - 1.0)
    bias = (pair_bias.astype(F32) + penalty[None, None, :]).astype(BF)
    hs = total_heads // 2
    bias_swap = row_swap(bias)
    first_shifts = row_shifts(bias[:hs])
    bias_swap, right_t = lax.optimization_barrier((bias_swap, jnp.transpose(right_proj, (2, 0, 1))))
    early = row_order(bias[:hs], bias_swap[:hs], first_shifts, row_shifts(bias_swap[:hs]))
    late = after(jnp.stack([bias[hs:], bias_swap[hs:]]), early)
    biases = [
        [(block[None], 0) for block in early],
        [(pair, z) for pair in [late] + row_shifts(late) for z in range(2)],
    ]

    quarter = rb // 4
    picks = [
        tuple(range(0, quarter)) + tuple(range(2 * quarter, 3 * quarter)),
        tuple(range(quarter, 2 * quarter)) + tuple(range(3 * quarter, rb)),
    ]

    def take(x, ids):
        return jnp.concatenate([x[ids[0] : ids[quarter - 1] + 1], x[ids[quarter] : ids[-1] + 1]])

    gathered = [
        lax.all_gather(jnp.concatenate([take(keys, ids), take(values, ids)]), "col", axis=0) for ids in picks
    ]
    small = [[take(a, ids) for a in (queries, gate_logits, out_grad, pair_cotangent)] for ids in picks]

    def attend(part, half, acc, earlier, order):
        q, g, do, pc = small[part]
        return attention(
            order, q, gathered[part], g, do, pc, query_weight, biases[half],
            acc, earlier, half * hs, hs, total_heads, part == 1,
        )

    a = attend(0, 0, None, None, order)
    b = attend(0, 1, None, list(a[:4]), order)
    gq0, gg0, dkv, car0 = b[:4]
    sum0 = lax.psum_scatter(dkv, "col", scatter_dimension=0)
    swap0 = row_swap(car0)
    c = attend(1, 0, a[-1], None, after(order, gq0))
    swap0, bias0 = lax.optimization_barrier((after(swap0, c[0]), c[-1]))
    pair0 = jnp.stack([car0, swap0])
    pairs0 = [pair0] + row_shifts(pair0)
    bias0 = row_parts(bias0)
    d = attend(1, 1, b[-1], list(c[:4]), after(order, pair0, c[0]))
    gq1, gg1, dkv, car1 = d[:4]
    sum1 = lax.psum_scatter(after(dkv, sum0), "col", scatter_dimension=0)
    pairs0, near0 = after((pairs0, bias0[1:4:2]), gq1)
    order_l, car1 = lax.optimization_barrier((order, car1))
    swap1 = row_swap(car1)
    left_a = left_product(after(order_l, pairs0), cols, pairs0, right_t, (0, 2))
    swap1, left_a = lax.optimization_barrier((swap1, left_a))
    pair1 = jnp.stack([car1, swap1])
    pairs1 = [pair1] + row_shifts(pair1)
    got_a = core_swap(left_a[1])
    left_b = left_product(after(order_l, pair1, left_a, sum0), cols, pairs0, right_t, (1, 3))
    far0, got_a, left_b, pairs1 = lax.optimization_barrier((bias0[2], got_a, left_b, pairs1))
    bias0 = add_all([bias0[0], far0] + list(near0))
    got_b = core_swap(left_b[1])
    pairs1, got_b, bias1 = lax.optimization_barrier((pairs1, got_b, d[-1]))
    part_l0 = jnp.concatenate([add_pair(left_a[0], got_a), add_pair(left_b[0], got_b)], axis=1)
    shifts_l0 = [x_shift(part_l0, dx) for dx in (1, 3, 2)]
    bias1 = row_parts(bias1)
    left_c = left_product(after(order, pairs1, part_l0), cols, pairs1, right_t, (0, 1, 2, 3))
    shifts_l0, bias1[1], bias1[3], left_c = lax.optimization_barrier((shifts_l0, bias1[1], bias1[3], left_c))
    got_c = core_swap(left_c[1])
    sum_l0 = add_all([part_l0[0:2]] + shifts_l0)
    part_l1 = add_pair(left_c[0], after(got_c, sum_l0))
    sum_l1 = add_all([part_l1[0:2]] + [x_shift(part_l1, dx) for dx in (1, 3, 2)])
    left = z_sum(jnp.concatenate([sum_l0, sum_l1], axis=1))
    bias1 = add_all(after(bias1, part_l1))
    bias_keep, bias_send = [jnp.concatenate([bias0[z], bias1[z]]) for z in range(2)]
    grad_bias = bias_keep.astype(F32) + row_swap(bias_send).astype(F32)
    sum0, sum1 = after((sum0, sum1), left)

    def untake(a, b):
        return jnp.concatenate([a[:quarter], b[:quarter], a[quarter:], b[quarter:]])

    gq, gg = untake(gq0, gq1), untake(gg0, gg1)
    dk, dv = untake(sum0[::2], sum1[::2]), untake(sum0[1::2], sum1[1::2])
    return (gq, dk, dv, gg, grad_bias, left)


def solution(mesh):
    in_specs = (
        P("row", "col", None),
        P("row", "col", None),
        P("row", "col", None),
        P("row", "col", None),
        P("row", "col", None),
        P(None, "col", "row"),
        P(),
        P(),
        P("row", "col", None),
        P("col", "row", None),
    )
    out_specs = (
        P("row", "col", None),
        P("row", "col", None),
        P("row", "col", None),
        P("row", "col", None),
        P(None, "col", "row"),
        P("col", "row", None),
    )
    return jax.shard_map(local, mesh=mesh, in_specs=in_specs, out_specs=out_specs, check_vma=False)
```

```python
import functools
import math

import jax
import jax.numpy as jnp
from jax import lax
from jax.experimental import pallas as pl
from jax.experimental.pallas import tpu as pltpu
from jax.sharding import PartitionSpec as P

F32 = jnp.float32
BF = jnp.bfloat16
NT = (((1,), (1,)), ((), ()))
NN = (((1,), (0,)), ((), ()))
LOG2E = 1.4426950408889634
VMEM_LIMIT = 60 * 1024 * 1024
big_penalty = 1000000000.0


def dot(a, b, dims=NN):
    return lax.dot_general(a, b, dims, preferred_element_type=F32)


def attention_kernel(h0, heads, total_heads, first, last, tile, order_ref, *refs):
    q_ref, k_ref, v_ref, g_ref, do_ref, pc_ref, w_ref = refs[:7]
    bias_refs = refs[7:15]
    refs = refs[15:]
    head_start = h0 == 0
    if not first:
        acc_in, refs = refs[0], refs[1:]
    if head_start:
        gq_ref, gg_ref, dkt_out, dvt_out, acc_out = refs[:5]
        refs = refs[5:]
    else:
        gq_in, gg_in, dkt_in, dvt_in = refs[:4]
        gq_ref, gg_ref, dkv_ref, car_ref, acc_out = refs[4:9]
        refs = refs[9:]
    bias_s, s_s, e_s, t_s = refs[:4]
    refs = refs[4:]
    if not head_start:
        dkt_s, dvt_s = refs[:2]
        refs = refs[2:]
    acc_s = acc_out
    if last:
        acc_s = refs[0]
        refs = refs[1:]
    i = pl.program_id(0)
    _, cj, chan = q_ref.shape
    head = chan // total_heads
    n = bias_s.shape[2]
    kb = n // 8
    scale = 1.0 / math.sqrt(head)
    tiles = n // tile
    fetch = None
    if not first:
        fetch = pltpu.make_async_copy(acc_in, acc_s, refs[0])

    @pl.when(i == 0)
    def _():
        if first:
            acc_s[...] = jnp.zeros(acc_s.shape, F32)
        else:
            fetch.start()
        for h in range(heads):
            for s in range(8):
                off = pl.multiple_of(order_ref[s] * kb, 128)
                bias_s[h, :, pl.ds(off, kb)] = bias_refs[s][0, h].astype(F32) * math.sqrt(head)

    def rows(ref, t):
        lo = t * tile
        out = []
        while lo < (t + 1) * tile:
            b, r = lo // cj, lo % cj
            m = min(cj - r, (t + 1) * tile - lo)
            out.append(ref[b, 0, r : r + m, :])
            lo += m
        return out[0] if len(out) == 1 else jnp.concatenate(out, axis=0)

    def lanes(h):
        lane = lax.broadcasted_iota(jnp.int32, (cj, chan), 1)
        return (lane >= (h0 + h) * head) & (lane < (h0 + h + 1) * head)

    def part(h):
        return slice((h0 + h) * head, (h0 + h + 1) * head)

    q = q_ref[0]
    q_t = q.astype(F32).T.astype(BF)
    tops = []
    for h in range(heads):
        qh = jnp.where(lanes(h), q, jnp.zeros_like(q))
        m = None
        for t in range(tiles):
            sl = slice(t * tile, (t + 1) * tile)
            s = dot(qh, rows(k_ref, t), NT) + bias_s[h, :, sl]
            s_s[h, :, sl] = s
            for u in range(tile // 128):
                p = s[:, u * 128 : (u + 1) * 128]
                m = p if m is None else jnp.maximum(m, p)
        tops.append(jnp.max(m, axis=1, keepdims=True))
    gate = jax.nn.sigmoid(g_ref[0].astype(F32))
    cot = do_ref[0].astype(F32)
    d_all = (cot * gate).astype(BF).astype(F32)
    gfac = cot * gate * (1.0 - gate)
    att_all = None
    stats = []
    for h in range(heads):
        lsum = None
        att = None
        for t in range(tiles):
            sl = slice(t * tile, (t + 1) * tile)
            e = jnp.exp2((s_s[h, :, sl] - tops[h]) * (scale * LOG2E))
            for u in range(tile // 128):
                p = e[:, u * 128 : (u + 1) * 128]
                lsum = p if lsum is None else lsum + p
            eb = e.astype(BF)
            e_s[h, :, sl] = eb
            a = dot(eb, rows(v_ref, t))
            att = a if att is None else att + a
        linv = 1.0 / jnp.sum(lsum, axis=1, keepdims=True)
        att = jnp.where(lanes(h), att * linv, 0.0)
        att_all = att if att_all is None else att_all + att
        delta = jnp.sum(d_all * att, axis=1, keepdims=True) * linv
        d_out = jnp.where(lanes(h), d_all * linv, 0.0)
        stats.append((delta, d_out.astype(BF)))
        t_s[h] = d_out.T.astype(BF)
    gg = gfac * att_all
    if not head_start:
        gg = gg + gg_in[0].astype(F32)
    gg_ref[0] = gg.astype(BF)

    if not first:

        @pl.when(i == 0)
        def _():
            fetch.wait()

    dq_all = None if head_start else gq_in[0].astype(F32)
    for h in range(heads):
        delta, dob = stats[h]
        out = slice(h * head, (h + 1) * head)
        do_t = t_s[h, part(h), :]
        dq = None
        for t in range(tiles):
            sl = slice(t * tile, (t + 1) * tile)
            dp = dot(dob, rows(v_ref, t), NT) - delta
            eb = e_s[h, :, sl]
            ds = eb.astype(F32) * dp
            acc_s[h, :, sl] += ds
            dsb = ds.astype(BF)
            a = dot(dsb, rows(k_ref, t))
            dq = a if dq is None else dq + a
            dk = dot(q_t[part(h), :], dsb) * scale
            dv = dot(do_t, eb)
            if head_start:
                dkt_out[0, out, sl] = dk.astype(BF)
                dvt_out[0, out, sl] = dv.astype(BF)
            else:
                dkt_s[out, sl] = dk
                dvt_s[out, sl] = dv
        dq = jnp.where(lanes(h), dq * scale, 0.0)
        dq_all = dq if dq_all is None else dq_all + dq
    gq = dq_all.astype(BF)
    gq_ref[0] = gq
    if not head_start:
        car = pc_ref[0].astype(F32) + dot(gq, w_ref[...], NT)
        car_ref[0] = car.T.astype(BF)
        for b in range(n // 384):
            sl = slice(b * 384, (b + 1) * 384)
            for j, old, new in ((0, dkt_in, dkt_s), (1, dvt_in, dvt_s)):
                both = jnp.concatenate([old[0, :, sl].astype(F32), new[:, sl]], axis=0).T.astype(BF)
                for c in range(384 // cj):
                    dkv_ref[(384 // cj) * b + c, j] = both[c * cj : (c + 1) * cj]

    if last:

        @pl.when(i == pl.num_programs(0) - 1)
        def _():
            for h in range(heads):
                for s in range(8):
                    off = pl.multiple_of(order_ref[s] * kb, 128)
                    acc_out[s, h] = acc_s[h, :, pl.ds(off, kb)].astype(BF)


def attention(order, q, kv, g, do, pc, w, biases, acc, earlier, h0, heads, total_heads, last, tile=3072):
    ni, cj, chan = q.shape
    nb = kv.shape[0]
    n = nb * cj
    kb = n // 8
    part = heads * (chan // total_heads)
    first = acc is None
    sd = jax.ShapeDtypeStruct

    def whole(*shape):
        return pl.BlockSpec(shape, lambda i, *r: (0,) * len(shape), pipeline_mode=pl.Buffered(1))

    per_row = pl.BlockSpec((1, cj, chan), lambda i, *r: (i, 0, 0))
    per_t = pl.BlockSpec((1, part, n), lambda i, *r: (i, 0, 0))
    k_spec = pl.BlockSpec((nb, 1, cj, chan), lambda i, *r: (0, i, 0, 0))
    v_spec = pl.BlockSpec((nb, 1, cj, chan), lambda i, *r: (0, ni + i, 0, 0))
    in_specs = [per_row, k_spec, v_spec, per_row, per_row, per_row, whole(chan, chan)]
    in_specs += [
        pl.BlockSpec((1, heads, cj, kb), lambda i, *r, z=z: (z, 0, 0, 0), pipeline_mode=pl.Buffered(1)) for _, z in biases
    ]
    ops = [q, kv, kv, g, do, pc, w, *(block for block, _ in biases)]
    if not first:
        in_specs.append(pl.BlockSpec(memory_space=pl.ANY))
        ops.append(acc)
    out_specs = [per_row, per_row]
    out_shape = [sd((ni, cj, chan), BF), sd((ni, cj, chan), BF)]
    scratch = [
        pltpu.VMEM((heads, cj, n), F32),
        pltpu.VMEM((heads, cj, n), F32),
        pltpu.VMEM((heads, cj, n), BF),
        pltpu.VMEM((heads, chan, cj), BF),
    ]
    if h0 == 0:
        out_specs += [per_t, per_t]
        out_shape += [sd((ni, part, n), BF), sd((ni, part, n), BF)]
    else:
        in_specs += [per_row, per_row, per_t, per_t]
        ops += earlier
        kv_out = pl.BlockSpec((nb, 2, cj, chan), lambda i, *r: (0, i, 0, 0))
        out_specs += [kv_out, pl.BlockSpec((1, chan, cj), lambda i, *r: (i, 0, 0))]
        out_shape += [sd((nb, 2 * ni, cj, chan), BF), sd((ni, chan, cj), BF)]
        scratch += [pltpu.VMEM((part, n), F32), pltpu.VMEM((part, n), F32)]
    if last:
        out_specs.append(whole(8, heads, cj, kb))
        out_shape.append(sd((8, heads, cj, kb), BF))
        scratch.append(pltpu.VMEM((heads, cj, n), F32))
    else:
        out_specs.append(whole(heads, cj, n))
        out_shape.append(sd((heads, cj, n), F32))
    if not first:
        scratch.append(pltpu.SemaphoreType.DMA(()))
    return pl.pallas_call(
        functools.partial(attention_kernel, h0, heads, total_heads, first, last, tile),
        grid_spec=pltpu.PrefetchScalarGridSpec(
            num_scalar_prefetch=1, grid=(ni,), in_specs=in_specs, out_specs=out_specs, scratch_shapes=scratch
        ),
        out_shape=out_shape,
        compiler_params=pltpu.CompilerParams(dimension_semantics=("arbitrary",), vmem_limit_bytes=VMEM_LIMIT),
        cost_estimate=pl.CostEstimate(
            flops=16 * heads * ni * cj * n * chan, bytes_accessed=30_000_000, transcendentals=heads * ni * cj * n
        ),
        name="attention_rows",
    )(order, *ops)


def left_kernel(order_ref, cols_ref, *refs):
    car = refs[:8]
    r_ref, keep_ref, send_ref, l_s, o_s = refs[8:]
    step = pl.program_id(0)
    _, ni, chan, cj = car[0].shape
    cb, _, kk = r_ref.shape
    half = ni // 2

    @pl.when(step == 0)
    def _():
        for s in range(8):
            for i in range(ni):
                at = pl.ds(pl.multiple_of((order_ref[s] * ni + i) * chan, chan), chan)
                x = car[s][0, i].astype(F32)
                l_s[0, at, :] = x[:, :128]
                l_s[1, at, : cj - 128] = x[:, 128:]

    for u in range(cb):
        c = step * cb + u
        a = l_s[0, pl.ds(c, 8 * ni, stride=chan), :]
        b = l_s[1, pl.ds(c, 8 * ni, stride=chan), :][:, : cj - 128]
        res = dot(jnp.concatenate([a, b], axis=1).astype(BF), r_ref[u])
        for b in range(kk // 128):
            o_s[b, pl.ds(c, 8 * ni, stride=chan), :] = res[:, b * 128 : (b + 1) * 128]

    @pl.when(step == pl.num_programs(0) - 1)
    def _():
        for r in range(8):
            for ref, col in ((keep_ref, cols_ref[r]), (send_ref, cols_ref[8 + r])):
                for i in range(half):
                    at = pl.ds(pl.multiple_of((col * half + i) * chan, chan), chan)
                    for b in range(kk // 128):
                        ref[r, i, b * 128 : (b + 1) * 128, :] = o_s[b, at, :].T.astype(BF)


def left_product(order, cols, pairs, right_t, cb=16):
    _, ni, chan, cj = pairs[0].shape
    kk = right_t.shape[2]

    def whole(*shape):
        return pl.BlockSpec(shape, lambda t, *r: (0,) * len(shape), pipeline_mode=pl.Buffered(1))

    cars = [
        pl.BlockSpec((1, ni, chan, cj), lambda t, *r, z=z: (z, 0, 0, 0), pipeline_mode=pl.Buffered(1))
        for _ in pairs
        for z in range(2)
    ]
    return pl.pallas_call(
        left_kernel,
        grid_spec=pltpu.PrefetchScalarGridSpec(
            num_scalar_prefetch=2,
            grid=(chan // cb,),
            in_specs=cars + [pl.BlockSpec((cb, cj, kk), lambda t, *r: (t, 0, 0))],
            out_specs=[whole(8, ni // 2, kk, chan)] * 2,
            scratch_shapes=[
                pltpu.VMEM((2, 8 * ni * chan, 128), F32),
                pltpu.VMEM((kk // 128, 8 * ni * chan, 128), F32),
            ],
        ),
        out_shape=[jax.ShapeDtypeStruct((8, ni // 2, kk, chan), BF)] * 2,
        compiler_params=pltpu.CompilerParams(dimension_semantics=("arbitrary",), vmem_limit_bytes=VMEM_LIMIT),
        cost_estimate=pl.CostEstimate(flops=40_000_000_000, bytes_accessed=30_000_000, transcendentals=0),
        name="left_product",
    )(order, cols, *(pair for pair in pairs for _ in range(2)), right_t)


def row_shift(x, dy):
    return lax.ppermute(x, "row", [(2 * y + z, 2 * ((y + dy) % 4) + z) for y in range(4) for z in range(2)])


def row_swap(x):
    return lax.ppermute(x, "row", [(r, r ^ 1) for r in range(8)])


def row_shifts(x):
    return [row_shift(x, dy) for dy in (1, 2, 3)]


def row_order(own, swapped, own_shifts, swapped_shifts):
    return [block for pair in zip([own] + own_shifts, [swapped] + swapped_shifts) for block in pair]


def row_parts(x):
    return [x[0:2]] + [row_shift(x[2 * dy : 2 * dy + 2], -dy) for dy in (1, 2, 3)]


def add_all(parts):
    return sum(p.astype(F32) for p in parts).astype(BF)


def core_swap(send):
    return lax.ppermute(send, "col", [(c, c ^ 1) for c in range(16)])


def add_pair(a, b):
    return (a.astype(F32) + b.astype(F32)).astype(BF)


def x_shift(part, dx):
    return lax.ppermute(part[2 * dx : 2 * dx + 2], "col", [(c, (c + 4 * dx) % 16) for c in range(16)])


def z_swap(total):
    return lax.ppermute(total[1], "col", [(c, c ^ 2) for c in range(16)])


def z_sum(total):
    return add_pair(total[0], z_swap(total))


def after(x, *done):
    return lax.optimization_barrier((x, done))[0]


def local(
    queries,
    keys,
    values,
    gate_logits,
    out_grad,
    pair_bias,
    residue_mask,
    query_weight,
    pair_cotangent,
    right_proj,
):
    total_heads = pair_bias.shape[0]
    kb = pair_bias.shape[2]
    rb = queries.shape[0]
    row = lax.axis_index("row")
    y, z = row // 2, row % 2
    order = jnp.stack([2 * ((y - s // 2 + 4) % 4) + (z ^ (s % 2)) for s in range(8)]).astype(jnp.int32)
    col = lax.axis_index("col")
    x, zl, core = col // 4, (col // 2) % 2, col % 2
    cols = jnp.stack(
        [((x + r % 8 // 2) % 4) * 4 + (zl ^ (r % 2)) * 2 + (core ^ (r // 8)) for r in range(16)]
    ).astype(jnp.int32)
    penalty = big_penalty * (lax.dynamic_slice_in_dim(residue_mask, row * kb, kb).astype(F32) - 1.0)
    bias = (pair_bias.astype(F32) + penalty[None, None, :]).astype(BF)
    hs = total_heads // 2
    bias_swap = row_swap(bias)
    first_shifts = row_shifts(bias[:hs])
    bias_swap, right_t = lax.optimization_barrier((bias_swap, jnp.transpose(right_proj, (2, 0, 1))))
    early = row_order(bias[:hs], bias_swap[:hs], first_shifts, row_shifts(bias_swap[:hs]))
    late = after(jnp.stack([bias[hs:], bias_swap[hs:]]), early)
    biases = [
        [(block[None], 0) for block in early],
        [(pair, z) for pair in [late] + row_shifts(late) for z in range(2)],
    ]

    quarter = rb // 4
    picks = [
        tuple(range(0, quarter)) + tuple(range(2 * quarter, 3 * quarter)),
        tuple(range(quarter, 2 * quarter)) + tuple(range(3 * quarter, rb)),
    ]

    def take(x, ids):
        return jnp.concatenate([x[ids[0] : ids[quarter - 1] + 1], x[ids[quarter] : ids[-1] + 1]])

    gathered = [
        lax.all_gather(jnp.concatenate([take(keys, ids), take(values, ids)]), "col", axis=0) for ids in picks
    ]
    small = [[take(a, ids) for a in (queries, gate_logits, out_grad, pair_cotangent)] for ids in picks]

    def attend(part, half, acc, earlier, order):
        q, g, do, pc = small[part]
        return attention(
            order, q, gathered[part], g, do, pc, query_weight, biases[half],
            acc, earlier, half * hs, hs, total_heads, part == 1,
        )

    a = attend(0, 0, None, None, order)
    b = attend(0, 1, None, list(a[:4]), order)
    gq0, gg0, dkv, car0 = b[:4]
    sum0 = lax.psum_scatter(dkv, "col", scatter_dimension=0)
    swap0 = row_swap(car0)
    c = attend(1, 0, a[-1], None, after(order, gq0))
    swap0, bias0 = lax.optimization_barrier((after(swap0, c[0]), c[-1]))
    pair0 = jnp.stack([car0, swap0])
    pairs0 = [pair0] + row_shifts(pair0)
    bias0 = row_parts(bias0)
    d = attend(1, 1, b[-1], list(c[:4]), after(order, pair0, c[0]))
    gq1, gg1, dkv, car1 = d[:4]
    sum1 = lax.psum_scatter(after(dkv, sum0), "col", scatter_dimension=0)
    pairs0, near0 = after((pairs0, bias0[1:4:2]), gq1)
    order_l, car1 = lax.optimization_barrier((order, car1))
    swap1 = row_swap(car1)
    left0 = left_product(after(order_l, pairs0, near0), cols, pairs0, right_t)
    swap1, far0, left0, sum0 = lax.optimization_barrier((swap1, bias0[2], left0, sum0))
    pair1 = jnp.stack([car1, swap1])
    pairs1 = [pair1] + row_shifts(pair1)
    part_l0 = add_pair(left0[0], core_swap(left0[1]))
    near_l0 = [x_shift(part_l0, 1), x_shift(part_l0, 3)]
    bias0 = add_all([bias0[0], far0] + list(near0))
    pairs1, near_l0, bias1, bias0 = lax.optimization_barrier((pairs1, near_l0, d[-1], bias0))
    far_l0 = x_shift(part_l0, 2)
    bias1 = row_parts(bias1)
    left1 = left_product(after(order, pairs1, near_l0), cols, pairs1, right_t)
    far_l0, bias1, left1 = lax.optimization_barrier((far_l0, bias1, left1))
    part_l1 = add_pair(left1[0], core_swap(left1[1]))
    shifts_l1 = [x_shift(part_l1, dx) for dx in (1, 3, 2)]
    sum_l0 = add_all([part_l0[0:2], far_l0] + near_l0)
    bias1 = add_all(bias1)
    bias_keep, bias_send = [jnp.concatenate([bias0[z], bias1[z]]) for z in range(2)]
    got_l0, got_bias = z_swap(sum_l0), row_swap(bias_send)
    sum_l1 = add_all([part_l1[0:2]] + shifts_l1)
    got_l1 = z_swap(sum_l1)
    left = jnp.concatenate([add_pair(sum_l0[0], got_l0), add_pair(sum_l1[0], got_l1)])
    got_bias, bias_keep = after((got_bias, bias_keep), got_l1)
    grad_bias = bias_keep.astype(F32) + got_bias.astype(F32)
    sum0, sum1 = after((sum0, sum1), left)

    def untake(a, b):
        return jnp.concatenate([a[:quarter], b[:quarter], a[quarter:], b[quarter:]])

    gq, gg = untake(gq0, gq1), untake(gg0, gg1)
    dk, dv = untake(sum0[::2], sum1[::2]), untake(sum0[1::2], sum1[1::2])
    return (gq, dk, dv, gg, grad_bias, left)


def solution(mesh):
    in_specs = (
        P("row", "col", None),
        P("row", "col", None),
        P("row", "col", None),
        P("row", "col", None),
        P("row", "col", None),
        P(None, "col", "row"),
        P(),
        P(),
        P("row", "col", None),
        P("col", "row", None),
    )
    out_specs = (
        P("row", "col", None),
        P("row", "col", None),
        P("row", "col", None),
        P("row", "col", None),
        P(None, "col", "row"),
        P("col", "row", None),
    )
    return jax.shard_map(local, mesh=mesh, in_specs=in_specs, out_specs=out_specs, check_vma=False)
```

```python
import functools
import math

import jax
import jax.numpy as jnp
from jax import lax
from jax.experimental import pallas as pl
from jax.experimental.pallas import tpu as pltpu
from jax.sharding import PartitionSpec as P

F32 = jnp.float32
BF = jnp.bfloat16
NT = (((1,), (1,)), ((), ()))
NN = (((1,), (0,)), ((), ()))
LOG2E = 1.4426950408889634
VMEM_LIMIT = 60 * 1024 * 1024
big_penalty = 1000000000.0


def dot(a, b, dims=NN):
    return lax.dot_general(a, b, dims, preferred_element_type=F32)


def attention_kernel(h0, heads, total_heads, first, last, tile, order_ref, *refs):
    q_ref, k_ref, v_ref, g_ref, do_ref, pc_ref, w_ref = refs[:7]
    bias_refs = refs[7:15]
    refs = refs[15:]
    head_start = h0 == 0
    if not first:
        acc_in, refs = refs[0], refs[1:]
    if head_start:
        gq_ref, gg_ref, dkt_out, dvt_out, acc_out = refs[:5]
        refs = refs[5:]
    else:
        gq_in, gg_in, dkt_in, dvt_in = refs[:4]
        gq_ref, gg_ref, dkv_ref, car_ref, acc_out = refs[4:9]
        refs = refs[9:]
    bias_s, s_s, e_s, t_s = refs[:4]
    refs = refs[4:]
    if not head_start:
        dkt_s, dvt_s = refs[:2]
        refs = refs[2:]
    acc_s = acc_out
    if last:
        acc_s = refs[0]
        refs = refs[1:]
    i = pl.program_id(0)
    _, cj, chan = q_ref.shape
    head = chan // total_heads
    n = bias_s.shape[2]
    kb = n // 8
    scale = 1.0 / math.sqrt(head)
    tiles = n // tile
    fetch = None
    if not first:
        fetch = pltpu.make_async_copy(acc_in, acc_s, refs[0])

    @pl.when(i == 0)
    def _():
        if first:
            acc_s[...] = jnp.zeros(acc_s.shape, F32)
        else:
            fetch.start()
        for h in range(heads):
            for s in range(8):
                off = pl.multiple_of(order_ref[s] * kb, 128)
                bias_s[h, :, pl.ds(off, kb)] = bias_refs[s][0, h].astype(F32) * math.sqrt(head)

    def rows(ref, t):
        lo = t * tile
        out = []
        while lo < (t + 1) * tile:
            b, r = lo // cj, lo % cj
            m = min(cj - r, (t + 1) * tile - lo)
            out.append(ref[b, 0, r : r + m, :])
            lo += m
        return out[0] if len(out) == 1 else jnp.concatenate(out, axis=0)

    def lanes(h):
        lane = lax.broadcasted_iota(jnp.int32, (cj, chan), 1)
        return (lane >= (h0 + h) * head) & (lane < (h0 + h + 1) * head)

    def part(h):
        return slice((h0 + h) * head, (h0 + h + 1) * head)

    q = q_ref[0]
    q_t = q.astype(F32).T.astype(BF)
    tops = []
    for h in range(heads):
        qh = jnp.where(lanes(h), q, jnp.zeros_like(q))
        m = None
        for t in range(tiles):
            sl = slice(t * tile, (t + 1) * tile)
            s = dot(qh, rows(k_ref, t), NT) + bias_s[h, :, sl]
            s_s[h, :, sl] = s
            for u in range(tile // 128):
                p = s[:, u * 128 : (u + 1) * 128]
                m = p if m is None else jnp.maximum(m, p)
        tops.append(jnp.max(m, axis=1, keepdims=True))
    gate = jax.nn.sigmoid(g_ref[0].astype(F32))
    cot = do_ref[0].astype(F32)
    d_all = (cot * gate).astype(BF).astype(F32)
    gfac = cot * gate * (1.0 - gate)
    att_all = None
    stats = []
    for h in range(heads):
        lsum = None
        att = None
        for t in range(tiles):
            sl = slice(t * tile, (t + 1) * tile)
            e = jnp.exp2((s_s[h, :, sl] - tops[h]) * (scale * LOG2E))
            for u in range(tile // 128):
                p = e[:, u * 128 : (u + 1) * 128]
                lsum = p if lsum is None else lsum + p
            eb = e.astype(BF)
            e_s[h, :, sl] = eb
            a = dot(eb, rows(v_ref, t))
            att = a if att is None else att + a
        linv = 1.0 / jnp.sum(lsum, axis=1, keepdims=True)
        att = jnp.where(lanes(h), att * linv, 0.0)
        att_all = att if att_all is None else att_all + att
        delta = jnp.sum(d_all * att, axis=1, keepdims=True) * linv
        d_out = jnp.where(lanes(h), d_all * linv, 0.0)
        stats.append((delta, d_out.astype(BF)))
        t_s[h] = d_out.T.astype(BF)
    gg = gfac * att_all
    if not head_start:
        gg = gg + gg_in[0].astype(F32)
    gg_ref[0] = gg.astype(BF)

    if not first:

        @pl.when(i == 0)
        def _():
            fetch.wait()

    dq_all = None if head_start else gq_in[0].astype(F32)
    for h in range(heads):
        delta, dob = stats[h]
        out = slice(h * head, (h + 1) * head)
        do_t = t_s[h, part(h), :]
        dq = None
        for t in range(tiles):
            sl = slice(t * tile, (t + 1) * tile)
            dp = dot(dob, rows(v_ref, t), NT) - delta
            eb = e_s[h, :, sl]
            ds = eb.astype(F32) * dp
            acc_s[h, :, sl] += ds
            dsb = ds.astype(BF)
            a = dot(dsb, rows(k_ref, t))
            dq = a if dq is None else dq + a
            dk = dot(q_t[part(h), :], dsb) * scale
            dv = dot(do_t, eb)
            if head_start:
                dkt_out[0, out, sl] = dk.astype(BF)
                dvt_out[0, out, sl] = dv.astype(BF)
            else:
                dkt_s[out, sl] = dk
                dvt_s[out, sl] = dv
        dq = jnp.where(lanes(h), dq * scale, 0.0)
        dq_all = dq if dq_all is None else dq_all + dq
    gq = dq_all.astype(BF)
    gq_ref[0] = gq
    if not head_start:
        car = pc_ref[0].astype(F32) + dot(gq, w_ref[...], NT)
        car_ref[0] = car.T.astype(BF)
        for b in range(n // 384):
            sl = slice(b * 384, (b + 1) * 384)
            for j, old, new in ((0, dkt_in, dkt_s), (1, dvt_in, dvt_s)):
                both = jnp.concatenate([old[0, :, sl].astype(F32), new[:, sl]], axis=0).T.astype(BF)
                for c in range(384 // cj):
                    dkv_ref[(384 // cj) * b + c, j] = both[c * cj : (c + 1) * cj]

    if last:

        @pl.when(i == pl.num_programs(0) - 1)
        def _():
            for h in range(heads):
                for s in range(8):
                    off = pl.multiple_of(order_ref[s] * kb, 128)
                    acc_out[s, h] = acc_s[h, :, pl.ds(off, kb)].astype(BF)


def attention(order, q, kv, g, do, pc, w, biases, acc, earlier, h0, heads, total_heads, last, tile=3072):
    ni, cj, chan = q.shape
    nb = kv.shape[0]
    n = nb * cj
    kb = n // 8
    part = heads * (chan // total_heads)
    first = acc is None
    sd = jax.ShapeDtypeStruct

    def whole(*shape):
        return pl.BlockSpec(shape, lambda i, *r: (0,) * len(shape), pipeline_mode=pl.Buffered(1))

    per_row = pl.BlockSpec((1, cj, chan), lambda i, *r: (i, 0, 0))
    per_t = pl.BlockSpec((1, part, n), lambda i, *r: (i, 0, 0))
    k_spec = pl.BlockSpec((nb, 1, cj, chan), lambda i, *r: (0, i, 0, 0))
    v_spec = pl.BlockSpec((nb, 1, cj, chan), lambda i, *r: (0, ni + i, 0, 0))
    in_specs = [per_row, k_spec, v_spec, per_row, per_row, per_row, whole(chan, chan)]
    in_specs += [
        pl.BlockSpec((1, heads, cj, kb), lambda i, *r, z=z: (z, 0, 0, 0), pipeline_mode=pl.Buffered(1)) for _, z in biases
    ]
    ops = [q, kv, kv, g, do, pc, w, *(block for block, _ in biases)]
    if not first:
        in_specs.append(pl.BlockSpec(memory_space=pl.ANY))
        ops.append(acc)
    out_specs = [per_row, per_row]
    out_shape = [sd((ni, cj, chan), BF), sd((ni, cj, chan), BF)]
    scratch = [
        pltpu.VMEM((heads, cj, n), F32),
        pltpu.VMEM((heads, cj, n), F32),
        pltpu.VMEM((heads, cj, n), BF),
        pltpu.VMEM((heads, chan, cj), BF),
    ]
    if h0 == 0:
        out_specs += [per_t, per_t]
        out_shape += [sd((ni, part, n), BF), sd((ni, part, n), BF)]
    else:
        in_specs += [per_row, per_row, per_t, per_t]
        ops += earlier
        kv_out = pl.BlockSpec((nb, 2, cj, chan), lambda i, *r: (0, i, 0, 0))
        out_specs += [kv_out, pl.BlockSpec((1, chan, cj), lambda i, *r: (i, 0, 0))]
        out_shape += [sd((nb, 2 * ni, cj, chan), BF), sd((ni, chan, cj), BF)]
        scratch += [pltpu.VMEM((part, n), F32), pltpu.VMEM((part, n), F32)]
    if last:
        out_specs.append(whole(8, heads, cj, kb))
        out_shape.append(sd((8, heads, cj, kb), BF))
        scratch.append(pltpu.VMEM((heads, cj, n), F32))
    else:
        out_specs.append(whole(heads, cj, n))
        out_shape.append(sd((heads, cj, n), F32))
    if not first:
        scratch.append(pltpu.SemaphoreType.DMA(()))
    return pl.pallas_call(
        functools.partial(attention_kernel, h0, heads, total_heads, first, last, tile),
        grid_spec=pltpu.PrefetchScalarGridSpec(
            num_scalar_prefetch=1, grid=(ni,), in_specs=in_specs, out_specs=out_specs, scratch_shapes=scratch
        ),
        out_shape=out_shape,
        compiler_params=pltpu.CompilerParams(dimension_semantics=("arbitrary",), vmem_limit_bytes=VMEM_LIMIT),
        cost_estimate=pl.CostEstimate(
            flops=16 * heads * ni * cj * n * chan, bytes_accessed=30_000_000, transcendentals=heads * ni * cj * n
        ),
        name="attention_rows",
    )(order, *ops)


def left_kernel(order_ref, cols_ref, *refs):
    car = refs[:8]
    r_ref, keep_ref, send_ref, l_s, o_s = refs[8:]
    step = pl.program_id(0)
    _, ni, chan, cj = car[0].shape
    cb, _, kk = r_ref.shape
    half = ni // 2

    @pl.when(step == 0)
    def _():
        for s in range(8):
            for i in range(ni):
                at = pl.ds(pl.multiple_of((order_ref[s] * ni + i) * chan, chan), chan)
                x = car[s][0, i].astype(F32)
                l_s[0, at, :] = x[:, :128]
                l_s[1, at, : cj - 128] = x[:, 128:]

    for u in range(cb):
        c = step * cb + u
        a = l_s[0, pl.ds(c, 8 * ni, stride=chan), :]
        b = l_s[1, pl.ds(c, 8 * ni, stride=chan), :][:, : cj - 128]
        res = dot(jnp.concatenate([a, b], axis=1).astype(BF), r_ref[u])
        for b in range(kk // 128):
            o_s[b, pl.ds(c, 8 * ni, stride=chan), :] = res[:, b * 128 : (b + 1) * 128]

    @pl.when(step == pl.num_programs(0) - 1)
    def _():
        for r in range(8):
            for ref, col in ((keep_ref, cols_ref[r]), (send_ref, cols_ref[8 + r])):
                for i in range(half):
                    at = pl.ds(pl.multiple_of((col * half + i) * chan, chan), chan)
                    for b in range(kk // 128):
                        ref[r, i, b * 128 : (b + 1) * 128, :] = o_s[b, at, :].T.astype(BF)


def left_product(order, cols, pairs, right_t, cb=16):
    _, ni, chan, cj = pairs[0].shape
    kk = right_t.shape[2]

    def whole(*shape):
        return pl.BlockSpec(shape, lambda t, *r: (0,) * len(shape), pipeline_mode=pl.Buffered(1))

    cars = [
        pl.BlockSpec((1, ni, chan, cj), lambda t, *r, z=z: (z, 0, 0, 0), pipeline_mode=pl.Buffered(1))
        for _ in pairs
        for z in range(2)
    ]
    return pl.pallas_call(
        left_kernel,
        grid_spec=pltpu.PrefetchScalarGridSpec(
            num_scalar_prefetch=2,
            grid=(chan // cb,),
            in_specs=cars + [pl.BlockSpec((cb, cj, kk), lambda t, *r: (t, 0, 0))],
            out_specs=[whole(8, ni // 2, kk, chan)] * 2,
            scratch_shapes=[
                pltpu.VMEM((2, 8 * ni * chan, 128), F32),
                pltpu.VMEM((kk // 128, 8 * ni * chan, 128), F32),
            ],
        ),
        out_shape=[jax.ShapeDtypeStruct((8, ni // 2, kk, chan), BF)] * 2,
        compiler_params=pltpu.CompilerParams(dimension_semantics=("arbitrary",), vmem_limit_bytes=VMEM_LIMIT),
        cost_estimate=pl.CostEstimate(flops=40_000_000_000, bytes_accessed=30_000_000, transcendentals=0),
        name="left_product",
    )(order, cols, *(pair for pair in pairs for _ in range(2)), right_t)


def row_shift(x, dy):
    return lax.ppermute(x, "row", [(2 * y + z, 2 * ((y + dy) % 4) + z) for y in range(4) for z in range(2)])


def row_swap(x):
    return lax.ppermute(x, "row", [(r, r ^ 1) for r in range(8)])


def row_shifts(x):
    return [row_shift(x, dy) for dy in (1, 2, 3)]


def row_order(own, swapped, own_shifts, swapped_shifts):
    return [block for pair in zip([own] + own_shifts, [swapped] + swapped_shifts) for block in pair]


def row_parts(x):
    return [x[0:2]] + [row_shift(x[2 * dy : 2 * dy + 2], -dy) for dy in (1, 2, 3)]


def add_all(parts):
    return sum(p.astype(F32) for p in parts).astype(BF)


def core_swap(send):
    return lax.ppermute(send, "col", [(c, c ^ 1) for c in range(16)])


def add_pair(a, b):
    return (a.astype(F32) + b.astype(F32)).astype(BF)


def x_shift(part, dx):
    return lax.ppermute(part[2 * dx : 2 * dx + 2], "col", [(c, (c + 4 * dx) % 16) for c in range(16)])


def z_swap(total):
    return lax.ppermute(total[1], "col", [(c, c ^ 2) for c in range(16)])


def z_sum(total):
    return add_pair(total[0], z_swap(total))


def z_first(part):
    part = part.reshape((4, 2) + part.shape[1:])
    got = lax.ppermute(part[:, 1], "col", [(c, c ^ 2) for c in range(16)])
    half = add_pair(part[:, 0], got)
    moved = [lax.ppermute(half[dx], "col", [(c, (c + 4 * dx) % 16) for c in range(16)]) for dx in (1, 3, 2)]
    return add_all([half[0]] + moved)


def after(x, *done):
    return lax.optimization_barrier((x, done))[0]


def local(
    queries,
    keys,
    values,
    gate_logits,
    out_grad,
    pair_bias,
    residue_mask,
    query_weight,
    pair_cotangent,
    right_proj,
):
    total_heads = pair_bias.shape[0]
    kb = pair_bias.shape[2]
    rb = queries.shape[0]
    row = lax.axis_index("row")
    y, z = row // 2, row % 2
    order = jnp.stack([2 * ((y - s // 2 + 4) % 4) + (z ^ (s % 2)) for s in range(8)]).astype(jnp.int32)
    col = lax.axis_index("col")
    x, zl, core = col // 4, (col // 2) % 2, col % 2
    cols = jnp.stack(
        [((x + r % 8 // 2) % 4) * 4 + (zl ^ (r % 2)) * 2 + (core ^ (r // 8)) for r in range(16)]
    ).astype(jnp.int32)
    penalty = big_penalty * (lax.dynamic_slice_in_dim(residue_mask, row * kb, kb).astype(F32) - 1.0)
    bias = (pair_bias.astype(F32) + penalty[None, None, :]).astype(BF)
    hs = total_heads // 2
    bias_swap = row_swap(bias)
    first_shifts = row_shifts(bias[:hs])
    bias_swap, right_t = lax.optimization_barrier((bias_swap, jnp.transpose(right_proj, (2, 0, 1))))
    early = row_order(bias[:hs], bias_swap[:hs], first_shifts, row_shifts(bias_swap[:hs]))
    late = after(jnp.stack([bias[hs:], bias_swap[hs:]]), early)
    biases = [
        [(block[None], 0) for block in early],
        [(pair, z) for pair in [late] + row_shifts(late) for z in range(2)],
    ]

    quarter = rb // 4
    picks = [
        tuple(range(0, quarter)) + tuple(range(2 * quarter, 3 * quarter)),
        tuple(range(quarter, 2 * quarter)) + tuple(range(3 * quarter, rb)),
    ]

    def take(x, ids):
        return jnp.concatenate([x[ids[0] : ids[quarter - 1] + 1], x[ids[quarter] : ids[-1] + 1]])

    gathered = [
        lax.all_gather(jnp.concatenate([take(keys, ids), take(values, ids)]), "col", axis=0) for ids in picks
    ]
    small = [[take(a, ids) for a in (queries, gate_logits, out_grad, pair_cotangent)] for ids in picks]

    def attend(part, half, acc, earlier, order):
        q, g, do, pc = small[part]
        return attention(
            order, q, gathered[part], g, do, pc, query_weight, biases[half],
            acc, earlier, half * hs, hs, total_heads, part == 1,
        )

    a = attend(0, 0, None, None, order)
    b = attend(0, 1, None, list(a[:4]), order)
    gq0, gg0, dkv, car0 = b[:4]
    sum0 = lax.psum_scatter(dkv, "col", scatter_dimension=0)
    swap0 = row_swap(car0)
    c = attend(1, 0, a[-1], None, after(order, gq0))
    swap0, bias0 = lax.optimization_barrier((after(swap0, c[0]), c[-1]))
    pair0 = jnp.stack([car0, swap0])
    pairs0 = [pair0] + row_shifts(pair0)
    bias0 = row_parts(bias0)
    d = attend(1, 1, b[-1], list(c[:4]), after(order, pair0, c[0]))
    gq1, gg1, dkv, car1 = d[:4]
    sum1 = lax.psum_scatter(after(dkv, sum0), "col", scatter_dimension=0)
    pairs0, near0 = after((pairs0, bias0[1:4:2]), gq1)
    order_l, car1 = lax.optimization_barrier((order, car1))
    swap1 = row_swap(car1)
    swap1, sum0, pairs0, near0 = lax.optimization_barrier((swap1, sum0, pairs0, near0))
    pair1 = jnp.stack([car1, swap1])
    pairs1 = [pair1] + row_shifts(pair1)
    left0 = left_product(after(order_l, pair1), cols, pairs0, right_t)
    pairs1, far0, left0, bias1 = lax.optimization_barrier((pairs1, bias0[2], left0, d[-1]))
    bias0 = add_all([bias0[0], far0] + list(near0))
    got_l0 = core_swap(left0[1])
    bias1 = row_parts(bias1)
    got_bias0 = row_swap(bias0[1])
    left1 = left_product(after(order, pairs1, bias0), cols, pairs1, right_t)
    got_l0, bias1[1], bias1[3], got_bias0, left1, late1 = lax.optimization_barrier(
        (got_l0, bias1[1], bias1[3], got_bias0, left1, d[-1])
    )
    bias1[2] = row_parts(late1)[2]
    got_l1 = core_swap(left1[1])
    part_l0 = add_pair(left0[0], got_l0)
    shifts_l0 = [x_shift(part_l0, dx) for dx in (1, 3, 2)]
    part_l1 = add_pair(left1[0], got_l1)
    bias1 = add_all(after(bias1, part_l1))
    sum_l1 = z_first(part_l1)
    sum_l0 = z_sum(add_all([part_l0[0:2]] + shifts_l0))
    left = jnp.concatenate([sum_l0, sum_l1])
    got_bias1 = after(row_swap(bias1[1]), sum_l1)
    grad_bias = jnp.concatenate(
        [bias0[0].astype(F32) + got_bias0.astype(F32), bias1[0].astype(F32) + got_bias1.astype(F32)]
    )
    sum0, sum1 = after((sum0, sum1), left)

    def untake(a, b):
        return jnp.concatenate([a[:quarter], b[:quarter], a[quarter:], b[quarter:]])

    gq, gg = untake(gq0, gq1), untake(gg0, gg1)
    dk, dv = untake(sum0[::2], sum1[::2]), untake(sum0[1::2], sum1[1::2])
    return (gq, dk, dv, gg, grad_bias, left)


def solution(mesh):
    in_specs = (
        P("row", "col", None),
        P("row", "col", None),
        P("row", "col", None),
        P("row", "col", None),
        P("row", "col", None),
        P(None, "col", "row"),
        P(),
        P(),
        P("row", "col", None),
        P("col", "row", None),
    )
    out_specs = (
        P("row", "col", None),
        P("row", "col", None),
        P("row", "col", None),
        P("row", "col", None),
        P(None, "col", "row"),
        P("col", "row", None),
    )
    return jax.shard_map(local, mesh=mesh, in_specs=in_specs, out_specs=out_specs, check_vma=False)
```

```python
import functools
import math

import jax
import jax.numpy as jnp
from jax import lax
from jax.experimental import pallas as pl
from jax.experimental.pallas import tpu as pltpu
from jax.sharding import PartitionSpec as P

F32 = jnp.float32
BF = jnp.bfloat16
NT = (((1,), (1,)), ((), ()))
NN = (((1,), (0,)), ((), ()))
LOG2E = 1.4426950408889634
VMEM_LIMIT = 60 * 1024 * 1024
big_penalty = 1000000000.0


def dot(a, b, dims=NN):
    return lax.dot_general(a, b, dims, preferred_element_type=F32)


def attention_kernel(h0, heads, total_heads, first, last, tile, order_ref, *refs):
    q_ref, k_ref, v_ref, g_ref, do_ref, pc_ref, w_ref = refs[:7]
    bias_refs = refs[7:15]
    refs = refs[15:]
    head_start = h0 == 0
    if not first:
        acc_in, refs = refs[0], refs[1:]
    if head_start:
        gq_ref, gg_ref, dkt_out, dvt_out, acc_out = refs[:5]
        refs = refs[5:]
    else:
        gq_in, gg_in, dkt_in, dvt_in = refs[:4]
        gq_ref, gg_ref, dkv_ref, car_ref, acc_out = refs[4:9]
        refs = refs[9:]
    bias_s, s_s, e_s, t_s = refs[:4]
    refs = refs[4:]
    if not head_start:
        dkt_s, dvt_s = refs[:2]
        refs = refs[2:]
    acc_s = acc_out
    if last:
        acc_s = refs[0]
        refs = refs[1:]
    i = pl.program_id(0)
    _, cj, chan = q_ref.shape
    head = chan // total_heads
    n = bias_s.shape[2]
    kb = n // 8
    scale = 1.0 / math.sqrt(head)
    tiles = n // tile
    fetch = None
    if not first:
        fetch = pltpu.make_async_copy(acc_in, acc_s, refs[0])

    @pl.when(i == 0)
    def _():
        if first:
            acc_s[...] = jnp.zeros(acc_s.shape, F32)
        else:
            fetch.start()
        for h in range(heads):
            for s in range(8):
                off = pl.multiple_of(order_ref[s] * kb, 128)
                bias_s[h, :, pl.ds(off, kb)] = bias_refs[s][0, h].astype(F32) * math.sqrt(head)

    def rows(ref, t):
        lo = t * tile
        out = []
        while lo < (t + 1) * tile:
            b, r = lo // cj, lo % cj
            m = min(cj - r, (t + 1) * tile - lo)
            out.append(ref[b, 0, r : r + m, :])
            lo += m
        return out[0] if len(out) == 1 else jnp.concatenate(out, axis=0)

    def lanes(h):
        lane = lax.broadcasted_iota(jnp.int32, (cj, chan), 1)
        return (lane >= (h0 + h) * head) & (lane < (h0 + h + 1) * head)

    def part(h):
        return slice((h0 + h) * head, (h0 + h + 1) * head)

    q = q_ref[0]
    q_t = q.astype(F32).T.astype(BF)
    tops = []
    for h in range(heads):
        qh = jnp.where(lanes(h), q, jnp.zeros_like(q))
        m = None
        for t in range(tiles):
            sl = slice(t * tile, (t + 1) * tile)
            s = dot(qh, rows(k_ref, t), NT) + bias_s[h, :, sl]
            s_s[h, :, sl] = s
            for u in range(tile // 128):
                p = s[:, u * 128 : (u + 1) * 128]
                m = p if m is None else jnp.maximum(m, p)
        tops.append(jnp.max(m, axis=1, keepdims=True))
    gate = jax.nn.sigmoid(g_ref[0].astype(F32))
    cot = do_ref[0].astype(F32)
    d_all = (cot * gate).astype(BF).astype(F32)
    gfac = cot * gate * (1.0 - gate)
    att_all = None
    stats = []
    for h in range(heads):
        lsum = None
        att = None
        for t in range(tiles):
            sl = slice(t * tile, (t + 1) * tile)
            e = jnp.exp2((s_s[h, :, sl] - tops[h]) * (scale * LOG2E))
            for u in range(tile // 128):
                p = e[:, u * 128 : (u + 1) * 128]
                lsum = p if lsum is None else lsum + p
            eb = e.astype(BF)
            e_s[h, :, sl] = eb
            a = dot(eb, rows(v_ref, t))
            att = a if att is None else att + a
        linv = 1.0 / jnp.sum(lsum, axis=1, keepdims=True)
        att = jnp.where(lanes(h), att * linv, 0.0)
        att_all = att if att_all is None else att_all + att
        delta = jnp.sum(d_all * att, axis=1, keepdims=True) * linv
        d_out = jnp.where(lanes(h), d_all * linv, 0.0)
        stats.append((delta, d_out.astype(BF)))
        t_s[h] = d_out.T.astype(BF)
    gg = gfac * att_all
    if not head_start:
        gg = gg + gg_in[0].astype(F32)
    gg_ref[0] = gg.astype(BF)

    if not first:

        @pl.when(i == 0)
        def _():
            fetch.wait()

    dq_all = None if head_start else gq_in[0].astype(F32)
    for h in range(heads):
        delta, dob = stats[h]
        out = slice(h * head, (h + 1) * head)
        do_t = t_s[h, part(h), :]
        dq = None
        for t in range(tiles):
            sl = slice(t * tile, (t + 1) * tile)
            dp = dot(dob, rows(v_ref, t), NT) - delta
            eb = e_s[h, :, sl]
            ds = eb.astype(F32) * dp
            acc_s[h, :, sl] += ds
            dsb = ds.astype(BF)
            a = dot(dsb, rows(k_ref, t))
            dq = a if dq is None else dq + a
            dk = dot(q_t[part(h), :], dsb) * scale
            dv = dot(do_t, eb)
            if head_start:
                dkt_out[0, out, sl] = dk.astype(BF)
                dvt_out[0, out, sl] = dv.astype(BF)
            else:
                dkt_s[out, sl] = dk
                dvt_s[out, sl] = dv
        dq = jnp.where(lanes(h), dq * scale, 0.0)
        dq_all = dq if dq_all is None else dq_all + dq
    gq = dq_all.astype(BF)
    gq_ref[0] = gq
    if not head_start:
        car = pc_ref[0].astype(F32) + dot(gq, w_ref[...], NT)
        car_ref[0] = car.T.astype(BF)
        for b in range(n // 384):
            sl = slice(b * 384, (b + 1) * 384)
            for j, old, new in ((0, dkt_in, dkt_s), (1, dvt_in, dvt_s)):
                both = jnp.concatenate([old[0, :, sl].astype(F32), new[:, sl]], axis=0).T.astype(BF)
                for c in range(384 // cj):
                    dkv_ref[(384 // cj) * b + c, j] = both[c * cj : (c + 1) * cj]

    if last:

        @pl.when(i == pl.num_programs(0) - 1)
        def _():
            for h in range(heads):
                for s in range(8):
                    off = pl.multiple_of(order_ref[s] * kb, 128)
                    acc_out[s, h] = acc_s[h, :, pl.ds(off, kb)].astype(BF)


def attention(order, q, kv, g, do, pc, w, biases, acc, earlier, h0, heads, total_heads, last, tile=3072):
    ni, cj, chan = q.shape
    nb = kv.shape[0]
    n = nb * cj
    kb = n // 8
    part = heads * (chan // total_heads)
    first = acc is None
    sd = jax.ShapeDtypeStruct

    def whole(*shape):
        return pl.BlockSpec(shape, lambda i, *r: (0,) * len(shape), pipeline_mode=pl.Buffered(1))

    per_row = pl.BlockSpec((1, cj, chan), lambda i, *r: (i, 0, 0))
    per_t = pl.BlockSpec((1, part, n), lambda i, *r: (i, 0, 0))
    k_spec = pl.BlockSpec((nb, 1, cj, chan), lambda i, *r: (0, i, 0, 0))
    v_spec = pl.BlockSpec((nb, 1, cj, chan), lambda i, *r: (0, ni + i, 0, 0))
    in_specs = [per_row, k_spec, v_spec, per_row, per_row, per_row, whole(chan, chan)]
    in_specs += [
        pl.BlockSpec((1, heads, cj, kb), lambda i, *r, z=z: (z, 0, 0, 0), pipeline_mode=pl.Buffered(1)) for _, z in biases
    ]
    ops = [q, kv, kv, g, do, pc, w, *(block for block, _ in biases)]
    if not first:
        in_specs.append(pl.BlockSpec(memory_space=pl.ANY))
        ops.append(acc)
    out_specs = [per_row, per_row]
    out_shape = [sd((ni, cj, chan), BF), sd((ni, cj, chan), BF)]
    scratch = [
        pltpu.VMEM((heads, cj, n), F32),
        pltpu.VMEM((heads, cj, n), F32),
        pltpu.VMEM((heads, cj, n), BF),
        pltpu.VMEM((heads, chan, cj), BF),
    ]
    if h0 == 0:
        out_specs += [per_t, per_t]
        out_shape += [sd((ni, part, n), BF), sd((ni, part, n), BF)]
    else:
        in_specs += [per_row, per_row, per_t, per_t]
        ops += earlier
        kv_out = pl.BlockSpec((nb, 2, cj, chan), lambda i, *r: (0, i, 0, 0))
        out_specs += [kv_out, pl.BlockSpec((1, chan, cj), lambda i, *r: (i, 0, 0))]
        out_shape += [sd((nb, 2 * ni, cj, chan), BF), sd((ni, chan, cj), BF)]
        scratch += [pltpu.VMEM((part, n), F32), pltpu.VMEM((part, n), F32)]
    if last:
        out_specs.append(whole(8, heads, cj, kb))
        out_shape.append(sd((8, heads, cj, kb), BF))
        scratch.append(pltpu.VMEM((heads, cj, n), F32))
    else:
        out_specs.append(whole(heads, cj, n))
        out_shape.append(sd((heads, cj, n), F32))
    if not first:
        scratch.append(pltpu.SemaphoreType.DMA(()))
    return pl.pallas_call(
        functools.partial(attention_kernel, h0, heads, total_heads, first, last, tile),
        grid_spec=pltpu.PrefetchScalarGridSpec(
            num_scalar_prefetch=1, grid=(ni,), in_specs=in_specs, out_specs=out_specs, scratch_shapes=scratch
        ),
        out_shape=out_shape,
        compiler_params=pltpu.CompilerParams(dimension_semantics=("arbitrary",), vmem_limit_bytes=VMEM_LIMIT),
        cost_estimate=pl.CostEstimate(
            flops=16 * heads * ni * cj * n * chan, bytes_accessed=30_000_000, transcendentals=heads * ni * cj * n
        ),
        name="attention_rows",
    )(order, *ops)


def left_kernel(order_ref, cols_ref, *refs):
    car = refs[:8]
    r_ref, keep_ref, send_ref, l_s, o_s = refs[8:]
    step = pl.program_id(0)
    _, ni, chan, cj = car[0].shape
    cb, _, kk = r_ref.shape
    half = ni // 2

    @pl.when(step == 0)
    def _():
        for s in range(8):
            for i in range(ni):
                at = pl.ds(pl.multiple_of((order_ref[s] * ni + i) * chan, chan), chan)
                x = car[s][0, i].astype(F32)
                l_s[0, at, :] = x[:, :128]
                l_s[1, at, : cj - 128] = x[:, 128:]

    for u in range(cb):
        c = step * cb + u
        a = l_s[0, pl.ds(c, 8 * ni, stride=chan), :]
        b = l_s[1, pl.ds(c, 8 * ni, stride=chan), :][:, : cj - 128]
        res = dot(jnp.concatenate([a, b], axis=1).astype(BF), r_ref[u])
        for b in range(kk // 128):
            o_s[b, pl.ds(c, 8 * ni, stride=chan), :] = res[:, b * 128 : (b + 1) * 128]

    @pl.when(step == pl.num_programs(0) - 1)
    def _():
        for r in range(8):
            for ref, col in ((keep_ref, cols_ref[r]), (send_ref, cols_ref[8 + r])):
                for i in range(half):
                    at = pl.ds(pl.multiple_of((col * half + i) * chan, chan), chan)
                    for b in range(kk // 128):
                        ref[r, i, b * 128 : (b + 1) * 128, :] = o_s[b, at, :].T.astype(BF)


def left_product(order, cols, pairs, right_t, cb=16):
    _, ni, chan, cj = pairs[0].shape
    kk = right_t.shape[2]

    def whole(*shape):
        return pl.BlockSpec(shape, lambda t, *r: (0,) * len(shape), pipeline_mode=pl.Buffered(1))

    cars = [
        pl.BlockSpec((1, ni, chan, cj), lambda t, *r, z=z: (z, 0, 0, 0), pipeline_mode=pl.Buffered(1))
        for _ in pairs
        for z in range(2)
    ]
    return pl.pallas_call(
        left_kernel,
        grid_spec=pltpu.PrefetchScalarGridSpec(
            num_scalar_prefetch=2,
            grid=(chan // cb,),
            in_specs=cars + [pl.BlockSpec((cb, cj, kk), lambda t, *r: (t, 0, 0))],
            out_specs=[whole(8, ni // 2, kk, chan)] * 2,
            scratch_shapes=[
                pltpu.VMEM((2, 8 * ni * chan, 128), F32),
                pltpu.VMEM((kk // 128, 8 * ni * chan, 128), F32),
            ],
        ),
        out_shape=[jax.ShapeDtypeStruct((8, ni // 2, kk, chan), BF)] * 2,
        compiler_params=pltpu.CompilerParams(dimension_semantics=("arbitrary",), vmem_limit_bytes=VMEM_LIMIT),
        cost_estimate=pl.CostEstimate(flops=40_000_000_000, bytes_accessed=30_000_000, transcendentals=0),
        name="left_product",
    )(order, cols, *(pair for pair in pairs for _ in range(2)), right_t)


def row_shift(x, dy):
    return lax.ppermute(x, "row", [(2 * y + z, 2 * ((y + dy) % 4) + z) for y in range(4) for z in range(2)])


def row_swap(x):
    return lax.ppermute(x, "row", [(r, r ^ 1) for r in range(8)])


def row_shifts(x):
    return [row_shift(x, dy) for dy in (1, 2, 3)]


def row_order(own, swapped, own_shifts, swapped_shifts):
    return [block for pair in zip([own] + own_shifts, [swapped] + swapped_shifts) for block in pair]


def row_parts(x):
    return [x[0:2]] + [row_shift(x[2 * dy : 2 * dy + 2], -dy) for dy in (1, 2, 3)]


def add_all(parts):
    return sum(p.astype(F32) for p in parts).astype(BF)


def core_swap(send):
    return lax.ppermute(send, "col", [(c, c ^ 1) for c in range(16)])


def add_pair(a, b):
    return (a.astype(F32) + b.astype(F32)).astype(BF)


def x_shift(part, dx):
    return lax.ppermute(part[2 * dx : 2 * dx + 2], "col", [(c, (c + 4 * dx) % 16) for c in range(16)])


def z_swap(total):
    return lax.ppermute(total[1], "col", [(c, c ^ 2) for c in range(16)])


def z_first(part):
    part = part.reshape((4, 2) + part.shape[1:])
    got = lax.ppermute(part[:, 1], "col", [(c, c ^ 2) for c in range(16)])
    half = add_pair(part[:, 0], got)
    moved = [lax.ppermute(half[dx], "col", [(c, (c + 4 * dx) % 16) for c in range(16)]) for dx in (1, 3, 2)]
    return add_all([half[0]] + moved)


def after(x, *done):
    return lax.optimization_barrier((x, done))[0]


def local(
    queries,
    keys,
    values,
    gate_logits,
    out_grad,
    pair_bias,
    residue_mask,
    query_weight,
    pair_cotangent,
    right_proj,
):
    total_heads = pair_bias.shape[0]
    kb = pair_bias.shape[2]
    rb = queries.shape[0]
    row = lax.axis_index("row")
    y, z = row // 2, row % 2
    order = jnp.stack([2 * ((y - s // 2 + 4) % 4) + (z ^ (s % 2)) for s in range(8)]).astype(jnp.int32)
    col = lax.axis_index("col")
    x, zl, core = col // 4, (col // 2) % 2, col % 2
    cols = jnp.stack(
        [((x + r % 8 // 2) % 4) * 4 + (zl ^ (r % 2)) * 2 + (core ^ (r // 8)) for r in range(16)]
    ).astype(jnp.int32)
    penalty = big_penalty * (lax.dynamic_slice_in_dim(residue_mask, row * kb, kb).astype(F32) - 1.0)
    bias = (pair_bias.astype(F32) + penalty[None, None, :]).astype(BF)
    hs = total_heads // 2
    bias_swap = row_swap(bias)
    first_shifts = row_shifts(bias[:hs])
    bias_swap, right_t = lax.optimization_barrier((bias_swap, jnp.transpose(right_proj, (2, 0, 1))))
    early = row_order(bias[:hs], bias_swap[:hs], first_shifts, row_shifts(bias_swap[:hs]))
    late = after(jnp.stack([bias[hs:], bias_swap[hs:]]), early)
    biases = [
        [(block[None], 0) for block in early],
        [(pair, z) for pair in [late] + row_shifts(late) for z in range(2)],
    ]

    quarter = rb // 4
    picks = [
        tuple(range(0, quarter)) + tuple(range(2 * quarter, 3 * quarter)),
        tuple(range(quarter, 2 * quarter)) + tuple(range(3 * quarter, rb)),
    ]

    def take(x, ids):
        return jnp.concatenate([x[ids[0] : ids[quarter - 1] + 1], x[ids[quarter] : ids[-1] + 1]])

    gathered = [
        lax.all_gather(jnp.concatenate([take(keys, ids), take(values, ids)]), "col", axis=0) for ids in picks
    ]
    small = [[take(a, ids) for a in (queries, gate_logits, out_grad, pair_cotangent)] for ids in picks]

    def attend(part, half, acc, earlier, order):
        q, g, do, pc = small[part]
        return attention(
            order, q, gathered[part], g, do, pc, query_weight, biases[half],
            acc, earlier, half * hs, hs, total_heads, part == 1,
        )

    a = attend(0, 0, None, None, order)
    b = attend(0, 1, None, list(a[:4]), order)
    gq0, gg0, dkv, car0 = b[:4]
    sum0 = lax.psum_scatter(dkv, "col", scatter_dimension=0)
    swap0 = row_swap(car0)
    order_c, swap0 = lax.optimization_barrier((order, swap0))
    pair0 = jnp.stack([car0, swap0])
    pairs0 = [pair0] + row_shifts(pair0)
    c = attend(1, 0, a[-1], None, after(order_c, pair0))
    pairs0, bias0 = lax.optimization_barrier((pairs0, c[-1]))
    bias0 = row_parts(bias0)
    left0 = left_product(order, cols, pairs0, right_t)
    bias0[1], bias0[3], left0 = lax.optimization_barrier((bias0[1], bias0[3], left0))
    part_l0 = add_pair(left0[0], core_swap(left0[1]))
    order_d, part_l0 = lax.optimization_barrier((order, part_l0))
    shifts_l0 = [x_shift(part_l0, dx) for dx in (1, 3, 2)]
    d = attend(1, 1, b[-1], list(c[:4]), order_d)
    gq1, gg1, dkv, car1 = d[:4]
    sum1 = lax.psum_scatter(after(dkv, sum0), "col", scatter_dimension=0)
    swap1 = row_swap(car1)
    shifts_l0, far0, swap1, late1, sum0 = lax.optimization_barrier((shifts_l0, bias0[2], swap1, d[-1], sum0))
    pair1 = jnp.stack([car1, swap1])
    pairs1 = [pair1] + row_shifts(pair1)
    sum_l0 = add_all([part_l0[0:2]] + shifts_l0)
    bias0 = add_all([bias0[0], bias0[1], bias0[3], far0])
    pairs1, sum_l0, bias0, late1 = lax.optimization_barrier((pairs1, sum_l0, bias0, late1))
    bias1 = row_parts(late1)
    got_l0, got_bias0 = z_swap(sum_l0), row_swap(bias0[1])
    left1 = left_product(after(order, pairs1), cols, pairs1, right_t)
    got_l0, got_bias0, bias1[1], bias1[3], left1 = lax.optimization_barrier(
        (got_l0, got_bias0, bias1[1], bias1[3], left1)
    )
    part_l1 = add_pair(left1[0], core_swap(left1[1]))
    bias1 = add_all(after(bias1, part_l1))
    sum_l1 = z_first(part_l1)
    left = jnp.concatenate([add_pair(sum_l0[0], got_l0), sum_l1])
    got_bias1 = after(row_swap(bias1[1]), sum_l1)
    grad_bias = jnp.concatenate(
        [bias0[0].astype(F32) + got_bias0.astype(F32), bias1[0].astype(F32) + got_bias1.astype(F32)]
    )
    sum0, sum1 = after((sum0, sum1), left)

    def untake(a, b):
        return jnp.concatenate([a[:quarter], b[:quarter], a[quarter:], b[quarter:]])

    gq, gg = untake(gq0, gq1), untake(gg0, gg1)
    dk, dv = untake(sum0[::2], sum1[::2]), untake(sum0[1::2], sum1[1::2])
    return (gq, dk, dv, gg, grad_bias, left)


def solution(mesh):
    in_specs = (
        P("row", "col", None),
        P("row", "col", None),
        P("row", "col", None),
        P("row", "col", None),
        P("row", "col", None),
        P(None, "col", "row"),
        P(),
        P(),
        P("row", "col", None),
        P("col", "row", None),
    )
    out_specs = (
        P("row", "col", None),
        P("row", "col", None),
        P("row", "col", None),
        P("row", "col", None),
        P(None, "col", "row"),
        P("col", "row", None),
    )
    return jax.shard_map(local, mesh=mesh, in_specs=in_specs, out_specs=out_specs, check_vma=False)
```

```python
import functools
import math

import jax
import jax.numpy as jnp
from jax import lax
from jax.experimental import pallas as pl
from jax.experimental.pallas import tpu as pltpu
from jax.sharding import PartitionSpec as P

F32 = jnp.float32
BF = jnp.bfloat16
NT = (((1,), (1,)), ((), ()))
NN = (((1,), (0,)), ((), ()))
LOG2E = 1.4426950408889634
VMEM_LIMIT = 60 * 1024 * 1024
big_penalty = 1000000000.0


def dot(a, b, dims=NN):
    return lax.dot_general(a, b, dims, preferred_element_type=F32)


def attention_kernel(h0, heads, total_heads, first, last, tile, order_ref, *refs):
    q_ref, k_ref, v_ref, g_ref, do_ref, pc_ref, w_ref = refs[:7]
    bias_refs = refs[7:15]
    refs = refs[15:]
    head_start = h0 == 0
    if not first:
        acc_in, refs = refs[0], refs[1:]
    if head_start:
        gq_ref, gg_ref, dkt_out, dvt_out, acc_out = refs[:5]
        refs = refs[5:]
    else:
        gq_in, gg_in, dkt_in, dvt_in = refs[:4]
        gq_ref, gg_ref, dkv_ref, car_ref, acc_out = refs[4:9]
        refs = refs[9:]
    bias_s, s_s, e_s, t_s = refs[:4]
    refs = refs[4:]
    if not head_start:
        dkt_s, dvt_s = refs[:2]
        refs = refs[2:]
    acc_s = acc_out
    if last:
        acc_s = refs[0]
        refs = refs[1:]
    i = pl.program_id(0)
    _, cj, chan = q_ref.shape
    head = chan // total_heads
    n = bias_s.shape[2]
    kb = n // 8
    scale = 1.0 / math.sqrt(head)
    tiles = n // tile
    fetch = None
    if not first:
        fetch = pltpu.make_async_copy(acc_in, acc_s, refs[0])

    @pl.when(i == 0)
    def _():
        if first:
            acc_s[...] = jnp.zeros(acc_s.shape, F32)
        else:
            fetch.start()
        for h in range(heads):
            for s in range(8):
                off = pl.multiple_of(order_ref[s] * kb, 128)
                bias_s[h, :, pl.ds(off, kb)] = bias_refs[s][0, h].astype(F32) * math.sqrt(head)

    def rows(ref, t):
        lo = t * tile
        out = []
        while lo < (t + 1) * tile:
            b, r = lo // cj, lo % cj
            m = min(cj - r, (t + 1) * tile - lo)
            out.append(ref[b, 0, r : r + m, :])
            lo += m
        return out[0] if len(out) == 1 else jnp.concatenate(out, axis=0)

    def lanes(h):
        lane = lax.broadcasted_iota(jnp.int32, (cj, chan), 1)
        return (lane >= (h0 + h) * head) & (lane < (h0 + h + 1) * head)

    def part(h):
        return slice((h0 + h) * head, (h0 + h + 1) * head)

    q = q_ref[0]
    q_t = q.astype(F32).T.astype(BF)
    tops = []
    for h in range(heads):
        qh = jnp.where(lanes(h), q, jnp.zeros_like(q))
        m = None
        for t in range(tiles):
            sl = slice(t * tile, (t + 1) * tile)
            s = dot(qh, rows(k_ref, t), NT) + bias_s[h, :, sl]
            s_s[h, :, sl] = s
            for u in range(tile // 128):
                p = s[:, u * 128 : (u + 1) * 128]
                m = p if m is None else jnp.maximum(m, p)
        tops.append(jnp.max(m, axis=1, keepdims=True))
    gate = jax.nn.sigmoid(g_ref[0].astype(F32))
    cot = do_ref[0].astype(F32)
    d_all = (cot * gate).astype(BF).astype(F32)
    gfac = cot * gate * (1.0 - gate)
    att_all = None
    stats = []
    for h in range(heads):
        lsum = None
        att = None
        for t in range(tiles):
            sl = slice(t * tile, (t + 1) * tile)
            e = jnp.exp2((s_s[h, :, sl] - tops[h]) * (scale * LOG2E))
            for u in range(tile // 128):
                p = e[:, u * 128 : (u + 1) * 128]
                lsum = p if lsum is None else lsum + p
            eb = e.astype(BF)
            e_s[h, :, sl] = eb
            a = dot(eb, rows(v_ref, t))
            att = a if att is None else att + a
        linv = 1.0 / jnp.sum(lsum, axis=1, keepdims=True)
        att = jnp.where(lanes(h), att * linv, 0.0)
        att_all = att if att_all is None else att_all + att
        delta = jnp.sum(d_all * att, axis=1, keepdims=True) * linv
        d_out = jnp.where(lanes(h), d_all * linv, 0.0)
        stats.append((delta, d_out.astype(BF)))
        t_s[h] = d_out.T.astype(BF)
    gg = gfac * att_all
    if not head_start:
        gg = gg + gg_in[0].astype(F32)
    gg_ref[0] = gg.astype(BF)

    if not first:

        @pl.when(i == 0)
        def _():
            fetch.wait()

    dq_all = None if head_start else gq_in[0].astype(F32)
    for h in range(heads):
        delta, dob = stats[h]
        out = slice(h * head, (h + 1) * head)
        do_t = t_s[h, part(h), :]
        dq = None
        for t in range(tiles):
            sl = slice(t * tile, (t + 1) * tile)
            dp = dot(dob, rows(v_ref, t), NT) - delta
            eb = e_s[h, :, sl]
            ds = eb.astype(F32) * dp
            acc_s[h, :, sl] += ds
            dsb = ds.astype(BF)
            a = dot(dsb, rows(k_ref, t))
            dq = a if dq is None else dq + a
            dk = dot(q_t[part(h), :], dsb) * scale
            dv = dot(do_t, eb)
            if head_start:
                dkt_out[0, out, sl] = dk.astype(BF)
                dvt_out[0, out, sl] = dv.astype(BF)
            else:
                dkt_s[out, sl] = dk
                dvt_s[out, sl] = dv
        dq = jnp.where(lanes(h), dq * scale, 0.0)
        dq_all = dq if dq_all is None else dq_all + dq
    gq = dq_all.astype(BF)
    gq_ref[0] = gq
    if not head_start:
        car = pc_ref[0].astype(F32) + dot(gq, w_ref[...], NT)
        car_ref[0] = car.T.astype(BF)
        for b in range(n // 384):
            sl = slice(b * 384, (b + 1) * 384)
            for j, old, new in ((0, dkt_in, dkt_s), (1, dvt_in, dvt_s)):
                both = jnp.concatenate([old[0, :, sl].astype(F32), new[:, sl]], axis=0).T.astype(BF)
                for c in range(384 // cj):
                    dkv_ref[(384 // cj) * b + c, j] = both[c * cj : (c + 1) * cj]

    if last:

        @pl.when(i == pl.num_programs(0) - 1)
        def _():
            for h in range(heads):
                for s in range(8):
                    off = pl.multiple_of(order_ref[s] * kb, 128)
                    acc_out[s, h] = acc_s[h, :, pl.ds(off, kb)].astype(BF)


def attention(order, q, kv, g, do, pc, w, biases, acc, earlier, h0, heads, total_heads, last, tile=3072):
    ni, cj, chan = q.shape
    nb = kv.shape[0]
    n = nb * cj
    kb = n // 8
    part = heads * (chan // total_heads)
    first = acc is None
    sd = jax.ShapeDtypeStruct

    def whole(*shape):
        return pl.BlockSpec(shape, lambda i, *r: (0,) * len(shape), pipeline_mode=pl.Buffered(1))

    per_row = pl.BlockSpec((1, cj, chan), lambda i, *r: (i, 0, 0))
    per_t = pl.BlockSpec((1, part, n), lambda i, *r: (i, 0, 0))
    k_spec = pl.BlockSpec((nb, 1, cj, chan), lambda i, *r: (0, i, 0, 0))
    v_spec = pl.BlockSpec((nb, 1, cj, chan), lambda i, *r: (0, ni + i, 0, 0))
    in_specs = [per_row, k_spec, v_spec, per_row, per_row, per_row, whole(chan, chan)]
    in_specs += [
        pl.BlockSpec((1, heads, cj, kb), lambda i, *r, z=z: (z, 0, 0, 0), pipeline_mode=pl.Buffered(1)) for _, z in biases
    ]
    ops = [q, kv, kv, g, do, pc, w, *(block for block, _ in biases)]
    if not first:
        in_specs.append(pl.BlockSpec(memory_space=pl.ANY))
        ops.append(acc)
    out_specs = [per_row, per_row]
    out_shape = [sd((ni, cj, chan), BF), sd((ni, cj, chan), BF)]
    scratch = [
        pltpu.VMEM((heads, cj, n), F32),
        pltpu.VMEM((heads, cj, n), F32),
        pltpu.VMEM((heads, cj, n), BF),
        pltpu.VMEM((heads, chan, cj), BF),
    ]
    if h0 == 0:
        out_specs += [per_t, per_t]
        out_shape += [sd((ni, part, n), BF), sd((ni, part, n), BF)]
    else:
        in_specs += [per_row, per_row, per_t, per_t]
        ops += earlier
        kv_out = pl.BlockSpec((nb, 2, cj, chan), lambda i, *r: (0, i, 0, 0))
        out_specs += [kv_out, pl.BlockSpec((1, chan, cj), lambda i, *r: (i, 0, 0))]
        out_shape += [sd((nb, 2 * ni, cj, chan), BF), sd((ni, chan, cj), BF)]
        scratch += [pltpu.VMEM((part, n), F32), pltpu.VMEM((part, n), F32)]
    if last:
        out_specs.append(whole(8, heads, cj, kb))
        out_shape.append(sd((8, heads, cj, kb), BF))
        scratch.append(pltpu.VMEM((heads, cj, n), F32))
    else:
        out_specs.append(whole(heads, cj, n))
        out_shape.append(sd((heads, cj, n), F32))
    if not first:
        scratch.append(pltpu.SemaphoreType.DMA(()))
    return pl.pallas_call(
        functools.partial(attention_kernel, h0, heads, total_heads, first, last, tile),
        grid_spec=pltpu.PrefetchScalarGridSpec(
            num_scalar_prefetch=1, grid=(ni,), in_specs=in_specs, out_specs=out_specs, scratch_shapes=scratch
        ),
        out_shape=out_shape,
        compiler_params=pltpu.CompilerParams(dimension_semantics=("arbitrary",), vmem_limit_bytes=VMEM_LIMIT),
        cost_estimate=pl.CostEstimate(
            flops=16 * heads * ni * cj * n * chan, bytes_accessed=30_000_000, transcendentals=heads * ni * cj * n
        ),
        name="attention_rows",
    )(order, *ops)


def left_kernel(order_ref, cols_ref, *refs):
    car = refs[:8]
    r_ref, keep_ref, send_ref, l_s, o_s = refs[8:]
    step = pl.program_id(0)
    _, ni, chan, cj = car[0].shape
    cb, _, kk = r_ref.shape
    half = ni // 2

    @pl.when(step == 0)
    def _():
        for s in range(8):
            for i in range(ni):
                at = pl.ds(pl.multiple_of((order_ref[s] * ni + i) * chan, chan), chan)
                x = car[s][0, i].astype(F32)
                l_s[0, at, :] = x[:, :128]
                l_s[1, at, : cj - 128] = x[:, 128:]

    for u in range(cb):
        c = step * cb + u
        a = l_s[0, pl.ds(c, 8 * ni, stride=chan), :]
        b = l_s[1, pl.ds(c, 8 * ni, stride=chan), :][:, : cj - 128]
        res = dot(jnp.concatenate([a, b], axis=1).astype(BF), r_ref[u])
        for b in range(kk // 128):
            o_s[b, pl.ds(c, 8 * ni, stride=chan), :] = res[:, b * 128 : (b + 1) * 128]

    @pl.when(step == pl.num_programs(0) - 1)
    def _():
        for r in range(8):
            for ref, col in ((keep_ref, cols_ref[r]), (send_ref, cols_ref[8 + r])):
                for i in range(half):
                    at = pl.ds(pl.multiple_of((col * half + i) * chan, chan), chan)
                    for b in range(kk // 128):
                        ref[r, i, b * 128 : (b + 1) * 128, :] = o_s[b, at, :].T.astype(BF)


def left_product(order, cols, pairs, right_t, cb=16):
    _, ni, chan, cj = pairs[0].shape
    kk = right_t.shape[2]

    def whole(*shape):
        return pl.BlockSpec(shape, lambda t, *r: (0,) * len(shape), pipeline_mode=pl.Buffered(1))

    cars = [
        pl.BlockSpec((1, ni, chan, cj), lambda t, *r, z=z: (z, 0, 0, 0), pipeline_mode=pl.Buffered(1))
        for _ in pairs
        for z in range(2)
    ]
    return pl.pallas_call(
        left_kernel,
        grid_spec=pltpu.PrefetchScalarGridSpec(
            num_scalar_prefetch=2,
            grid=(chan // cb,),
            in_specs=cars + [pl.BlockSpec((cb, cj, kk), lambda t, *r: (t, 0, 0))],
            out_specs=[whole(8, ni // 2, kk, chan)] * 2,
            scratch_shapes=[
                pltpu.VMEM((2, 8 * ni * chan, 128), F32),
                pltpu.VMEM((kk // 128, 8 * ni * chan, 128), F32),
            ],
        ),
        out_shape=[jax.ShapeDtypeStruct((8, ni // 2, kk, chan), BF)] * 2,
        compiler_params=pltpu.CompilerParams(dimension_semantics=("arbitrary",), vmem_limit_bytes=VMEM_LIMIT),
        cost_estimate=pl.CostEstimate(flops=40_000_000_000, bytes_accessed=30_000_000, transcendentals=0),
        name="left_product",
    )(order, cols, *(pair for pair in pairs for _ in range(2)), right_t)


def row_shift(x, dy):
    return lax.ppermute(x, "row", [(2 * y + z, 2 * ((y + dy) % 4) + z) for y in range(4) for z in range(2)])


def row_swap(x):
    return lax.ppermute(x, "row", [(r, r ^ 1) for r in range(8)])


def row_shifts(x):
    return [row_shift(x, dy) for dy in (1, 2, 3)]


def row_order(own, swapped, own_shifts, swapped_shifts):
    return [block for pair in zip([own] + own_shifts, [swapped] + swapped_shifts) for block in pair]


def row_parts(x):
    return [x[0:2]] + [row_shift(x[2 * dy : 2 * dy + 2], -dy) for dy in (1, 2, 3)]


def add_all(parts):
    return sum(p.astype(F32) for p in parts).astype(BF)


def core_swap(send):
    return lax.ppermute(send, "col", [(c, c ^ 1) for c in range(16)])


def add_pair(a, b):
    return (a.astype(F32) + b.astype(F32)).astype(BF)


def x_shift(part, dx):
    return lax.ppermute(part[2 * dx : 2 * dx + 2], "col", [(c, (c + 4 * dx) % 16) for c in range(16)])


def z_swap(total):
    return lax.ppermute(total[1], "col", [(c, c ^ 2) for c in range(16)])


def z_first(part):
    part = part.reshape((4, 2) + part.shape[1:])
    got = lax.ppermute(part[:, 1], "col", [(c, c ^ 2) for c in range(16)])
    half = add_pair(part[:, 0], got)
    moved = [lax.ppermute(half[dx], "col", [(c, (c + 4 * dx) % 16) for c in range(16)]) for dx in (1, 3, 2)]
    return add_all([half[0]] + moved)


def after(x, *done):
    return lax.optimization_barrier((x, done))[0]


def local(
    queries,
    keys,
    values,
    gate_logits,
    out_grad,
    pair_bias,
    residue_mask,
    query_weight,
    pair_cotangent,
    right_proj,
):
    total_heads = pair_bias.shape[0]
    kb = pair_bias.shape[2]
    rb = queries.shape[0]
    row = lax.axis_index("row")
    y, z = row // 2, row % 2
    order = jnp.stack([2 * ((y - s // 2 + 4) % 4) + (z ^ (s % 2)) for s in range(8)]).astype(jnp.int32)
    col = lax.axis_index("col")
    x, zl, core = col // 4, (col // 2) % 2, col % 2
    cols = jnp.stack(
        [((x + r % 8 // 2) % 4) * 4 + (zl ^ (r % 2)) * 2 + (core ^ (r // 8)) for r in range(16)]
    ).astype(jnp.int32)
    penalty = big_penalty * (lax.dynamic_slice_in_dim(residue_mask, row * kb, kb).astype(F32) - 1.0)
    bias = (pair_bias.astype(F32) + penalty[None, None, :]).astype(BF)
    hs = total_heads // 2
    bias_swap = row_swap(bias)
    first_shifts = row_shifts(bias[:hs])
    bias_swap, right_t = lax.optimization_barrier((bias_swap, jnp.transpose(right_proj, (2, 0, 1))))
    early = row_order(bias[:hs], bias_swap[:hs], first_shifts, row_shifts(bias_swap[:hs]))
    late = after(jnp.stack([bias[hs:], bias_swap[hs:]]), early)
    biases = [
        [(block[None], 0) for block in early],
        [(pair, z) for pair in [late] + row_shifts(late) for z in range(2)],
    ]

    quarter = rb // 4
    picks = [
        tuple(range(0, quarter)) + tuple(range(2 * quarter, 3 * quarter)),
        tuple(range(quarter, 2 * quarter)) + tuple(range(3 * quarter, rb)),
    ]

    def take(x, ids):
        return jnp.concatenate([x[ids[0] : ids[quarter - 1] + 1], x[ids[quarter] : ids[-1] + 1]])

    gathered = [
        lax.all_gather(jnp.concatenate([take(keys, ids), take(values, ids)]), "col", axis=0) for ids in picks
    ]
    small = [[take(a, ids) for a in (queries, gate_logits, out_grad, pair_cotangent)] for ids in picks]

    def attend(part, half, acc, earlier, order):
        q, g, do, pc = small[part]
        return attention(
            order, q, gathered[part], g, do, pc, query_weight, biases[half],
            acc, earlier, half * hs, hs, total_heads, part == 1,
        )

    a = attend(0, 0, None, None, order)
    b = attend(0, 1, None, list(a[:4]), order)
    gq0, gg0, dkv, car0 = b[:4]
    sum0 = lax.psum_scatter(dkv, "col", scatter_dimension=0)
    swap0 = row_swap(car0)
    order_c, swap0 = lax.optimization_barrier((order, swap0))
    pair0 = jnp.stack([car0, swap0])
    pairs0 = [pair0] + row_shifts(pair0)
    c = attend(1, 0, a[-1], None, after(order_c, pair0))
    pairs0, bias0 = lax.optimization_barrier((pairs0, c[-1]))
    bias0 = row_parts(bias0)
    left0 = left_product(order, cols, pairs0, right_t)
    bias0[1], bias0[3], left0 = lax.optimization_barrier((bias0[1], bias0[3], left0))
    part_l0 = add_pair(left0[0], core_swap(left0[1]))
    order_d, part_l0 = lax.optimization_barrier((order, part_l0))
    shifts_l0 = [x_shift(part_l0, dx) for dx in (1, 3, 2)]
    d = attend(1, 1, b[-1], list(c[:4]), order_d)
    gq1, gg1 = d[:2]
    shifts_l0, far0, dkv, car1, late1 = lax.optimization_barrier((shifts_l0, bias0[2], d[2], d[3], d[-1]))
    sum1 = lax.psum_scatter(after(dkv, sum0), "col", scatter_dimension=0)
    swap1 = row_swap(car1)
    swap1, sum0 = lax.optimization_barrier((swap1, sum0))
    pair1 = jnp.stack([car1, swap1])
    pairs1 = [pair1] + row_shifts(pair1)
    sum_l0 = add_all([part_l0[0:2]] + shifts_l0)
    bias0 = add_all([bias0[0], bias0[1], bias0[3], far0])
    pairs1, sum_l0, bias0, late1 = lax.optimization_barrier((pairs1, sum_l0, bias0, late1))
    bias1 = row_parts(late1)
    got_l0, got_bias0 = z_swap(sum_l0), row_swap(bias0[1])
    left1 = left_product(after(order, pairs1), cols, pairs1, right_t)
    got_l0, got_bias0, bias1, left1 = lax.optimization_barrier((got_l0, got_bias0, bias1, left1))
    part_l1 = add_pair(left1[0], core_swap(left1[1]))
    bias1 = add_all(bias1)
    sum_l1 = z_first(part_l1)
    left = jnp.concatenate([add_pair(sum_l0[0], got_l0), sum_l1])
    got_bias1 = after(row_swap(bias1[1]), sum_l1)
    grad_bias = jnp.concatenate(
        [bias0[0].astype(F32) + got_bias0.astype(F32), bias1[0].astype(F32) + got_bias1.astype(F32)]
    )
    sum0, sum1 = after((sum0, sum1), left)

    def untake(a, b):
        return jnp.concatenate([a[:quarter], b[:quarter], a[quarter:], b[quarter:]])

    gq, gg = untake(gq0, gq1), untake(gg0, gg1)
    dk, dv = untake(sum0[::2], sum1[::2]), untake(sum0[1::2], sum1[1::2])
    return (gq, dk, dv, gg, grad_bias, left)


def solution(mesh):
    in_specs = (
        P("row", "col", None),
        P("row", "col", None),
        P("row", "col", None),
        P("row", "col", None),
        P("row", "col", None),
        P(None, "col", "row"),
        P(),
        P(),
        P("row", "col", None),
        P("col", "row", None),
    )
    out_specs = (
        P("row", "col", None),
        P("row", "col", None),
        P("row", "col", None),
        P("row", "col", None),
        P(None, "col", "row"),
        P("col", "row", None),
    )
    return jax.shard_map(local, mesh=mesh, in_specs=in_specs, out_specs=out_specs, check_vma=False)
```
